32 devices in a mesh: grp: 2 (over x), rows: 4 (over y, core), chan: 4 (over z).
Axes of the slice: x: 2, y: 2, z: 4, core: 2. Of those that a mesh axis runs over, the one named last changes fastest.
Arguments:
- frames_in: bfloat16 [512, 4, 16, 96], P('chan', None, ('grp', 'rows')), parts along dimension 2, may hold values from -48 to 48
- cache_first: bfloat16 [512, 2, 16, 96], P('chan', None, ('grp', 'rows')), parts along dimension 2, may hold values from -6 to 6
- gain_first: float32 [512], P('chan'), may hold values from 0.1 to 1.9
- shift_first: float32 [512], P('chan'), may hold values from -3 to 3
- kernel_first: bfloat16 [3, 3, 3, 512, 512], P(None, None, None, 'chan'), may hold values from -0.0625 to 0.0625
- bias_first: float32 [512], P('chan'), may hold values from -3 to 3
- cache_second: bfloat16 [512, 2, 16, 96], P('chan', None, ('grp', 'rows')), parts along dimension 2, may hold values from -6 to 6
- gain_second: float32 [512], P('chan'), may hold values from 0.1 to 1.9
- shift_second: float32 [512], P('chan'), may hold values from -3 to 3
- kernel_second: bfloat16 [3, 3, 3, 512, 512], P(None, None, None, 'chan'), may hold values from -0.0625 to 0.0625
- bias_second: float32 [512], P('chan'), may hold values from -3 to 3
Outputs:
- decoded: bfloat16 [512, 4, 16, 96], P('chan', None, ('grp', 'rows')), parts along dimension 2
- next_cache: bfloat16 [512, 2, 16, 96], P('chan', None, ('grp', 'rows')), parts along dimension 2
The draws below stay inside these ranges and needn't reach their ends.
There are 2 independent parts, one for each index of `grp`. The reference program is written for one: setup_inputs(seed, part) draws one part's arguments, and reference() takes and returns one part's arrays. A program takes and returns all parts, laid end to end along the dimension named above; an argument that names none is the same for every part. Nothing has to cross between parts.
All inputs are finite; a program needn't handle non-finite values.
Results may differ from the reference program's by a relative error of at most 0.009.
Values may be sent and summed in bfloat16 or wider, within the bound.
A program may use at most 128 MiB of HBM per device.

```python
import math
import jax
import jax.numpy as jnp
from jax import lax

CHANNELS = 512
GROUPS = 32
FRAMES = 4
WIDTH = 96
HEIGHT = 8


def draw_frames_in(key, part):
    keys = jax.random.split(key, 6)
    shape_full = (CHANNELS, FRAMES, HEIGHT, WIDTH)
    ramp = jnp.linspace(-1.0, 1.0, HEIGHT)
    direction = (2 * jax.random.randint(keys[3], (), 0, 2) - 1).astype(jnp.float32)
    slope = direction * jax.random.uniform(keys[4], (), minval=0.6, maxval=1.0)
    rough = jax.random.uniform(keys[5], (HEIGHT,), minval=-1.0, maxval=1.0)
    level = jnp.clip(0.5 + 0.35 * slope * ramp + 0.25 * rough, 0.0, 1.0)
    row_scale = jnp.exp(math.log(3.0) * level)
    col_scale = jnp.exp(jax.random.uniform(keys[0], (WIDTH,), minval=0.0, maxval=math.log(3.4)))
    base = jax.random.normal(keys[1], shape_full)
    values = base * row_scale[None, None, :, None] * col_scale[None, None, None, :]
    return jnp.clip(values, -48.0, 48.0).astype(jnp.bfloat16)


def raised(array, key, source, target, parts, factor):
    owner, partner = [(jnp.arange(array.shape[dim]) // (array.shape[dim] // parts)).reshape([-1 if axis == dim else 1 for axis in range(array.ndim)]) for dim in (source, target)]
    chosen = jax.random.permutation(key, parts)[partner]
    strong = (owner == chosen) | (owner == (partner + parts // 2) % parts)
    return jnp.where(strong, factor * array, array)


def block_levels(rng, extent, shards, least, largest):
    level, own = 1.0, jax.random.fold_in(rng, 6)
    for position, shards_of in shards:
        steps = jnp.exp(jax.random.uniform(jax.random.fold_in(own, position), (shards_of,), jnp.float32, least / len(shards), largest / len(shards)))
        level = level * jnp.repeat(steps, extent[position] // shards_of).reshape([-1 if axis == position else 1 for axis in range(len(extent))])
    return level


def bell_draw(rng, shape, spread, reach, cuts=(), held_as=jnp.bfloat16):
    loudness = block_levels(rng, shape, cuts, -0.22, 0.18) if cuts else 1.0
    entries = jax.random.normal(rng, shape, jnp.float32) * spread * loudness
    return jnp.minimum(jnp.maximum(entries, -reach), reach).astype(held_as)


def noise_with(rng, extent, deviation, reach, cuts, heavy, dtype=jnp.bfloat16):
    values = deviation * jax.random.normal(rng, extent, jnp.float32)
    if cuts:
        values = values * block_levels(rng, extent, cuts, -0.22, 0.18)
    return jnp.clip(raised(values, jax.random.fold_in(rng, 3), *heavy), -reach, reach).astype(dtype)


def setup_inputs(seed: int = 0, part: int = 0) -> dict:
    key_list = jax.random.split(jax.random.key(seed), 12)
    part_keys = jax.random.split(jax.random.fold_in(key_list[11], part), 12)
    return {
        "frames_in": draw_frames_in(jax.random.fold_in(jax.random.fold_in(key_list[11], part), 71), part),
        "cache_first": bell_draw(part_keys[1], (CHANNELS, 2, HEIGHT, WIDTH), 1.0, 6.0, ((0, 4), (2, 4))),
        "gain_first": jnp.clip(1.0 + 0.18 * jax.random.normal(key_list[2], (CHANNELS,), jnp.float32), 0.1, 1.9),
        "shift_first": bell_draw(key_list[3], (CHANNELS,), 0.5, 3.0, ((0, 4),), jnp.float32),
        "kernel_first": noise_with(key_list[4], (3, 3, 3, CHANNELS, CHANNELS), (27 * CHANNELS) ** -0.5, 0.0625, ((3, 4),), (3, 4, 4, 2.0)),
        "bias_first": bell_draw(key_list[5], (CHANNELS,), 0.5, 3.0, ((0, 4),), jnp.float32),
        "cache_second": bell_draw(part_keys[6], (CHANNELS, 2, HEIGHT, WIDTH), 1.0, 6.0, ((0, 4), (2, 4))),
        "gain_second": jnp.clip(1.0 + 0.18 * jax.random.normal(key_list[7], (CHANNELS,), jnp.float32), 0.1, 1.9),
        "shift_second": bell_draw(key_list[8], (CHANNELS,), 0.5, 3.0, ((0, 4),), jnp.float32),
        "kernel_second": noise_with(key_list[9], (3, 3, 3, CHANNELS, CHANNELS), (27 * CHANNELS) ** -0.5, 0.0625, ((3, 4),), (3, 4, 4, 2.0)),
        "bias_second": bell_draw(key_list[10], (CHANNELS,), 0.5, 3.0, ((0, 4),), jnp.float32),
    }


def norm_act(values, gain, shift):
    grouped = values.reshape(GROUPS, -1)
    average = lax.optimization_barrier(jnp.mean(grouped, axis=1, keepdims=True))
    squares = lax.optimization_barrier(jnp.mean(grouped * grouped, axis=1, keepdims=True))
    scaled = ((grouped - average) * lax.rsqrt(squares - average * average + 1e-06)).reshape(values.shape)
    affine = scaled * gain[:, None, None, None] + shift[:, None, None, None]
    return jax.nn.silu(affine).astype(jnp.bfloat16)

def causal_conv(history, current, kernel, bias):
    joined = jnp.concatenate([history, current], axis=1).astype(jnp.float32)[None]
    result = lax.conv_general_dilated(joined, kernel.astype(jnp.float32), (1, 1, 1), [(0, 0), (1, 1), (1, 1)], dimension_numbers=('NCDHW', 'DHWIO', 'NCDHW'), precision=lax.Precision.HIGHEST)
    return result[0] + bias[:, None, None, None]

def reference(frames_in, cache_first, gain_first, shift_first, kernel_first, bias_first, cache_second, gain_second, shift_second, kernel_second, bias_second):
    activated = norm_act(frames_in.astype(jnp.float32), gain_first, shift_first)
    hidden = causal_conv(cache_first, activated, kernel_first, bias_first).astype(jnp.bfloat16)
    second = norm_act(hidden.astype(jnp.float32), gain_second, shift_second)
    decoded = causal_conv(cache_second, second, kernel_second, bias_second).astype(jnp.bfloat16)
    return (decoded, second[:, FRAMES - 2:])
```

```python
import functools

import jax
import jax.numpy as jnp
from jax import lax
from jax.experimental import pallas as pl
from jax.experimental.pallas import tpu as pltpu
from jax.sharding import PartitionSpec as P

GROUPS = 32
MESH = pl.DeviceIdType.MESH
F32 = jnp.float32
BF16 = jnp.bfloat16


def kernel(
    nr, nc, channels,
    x_hbm, c1_hbm, g1, s1, k1_hbm, b1, c2_hbm, g2, s2, k2_hbm, b2,
    out_ref, next_ref,
    xv, cv, hid, w, x9, halo, mom, part, snd, rcv,
    loc_sem, mom_send, mom_recv, halo_send, halo_recv, rs_send, rs_recv,
):
    frames, band, width, ch = xv.shape
    past = cv.shape[1]
    taps = 9 * ch
    cells = frames * band * width
    r = lax.axis_index("rows")
    c = lax.axis_index("chan")

    loads = [
        pltpu.make_async_copy(src, dst, loc_sem.at[i])
        for i, (src, dst) in enumerate((
            (x_hbm, xv), (c1_hbm, cv.at[0]), (k1_hbm, w.at[0]),
            (c2_hbm, cv.at[1]), (k2_hbm, w.at[1]),
        ))
    ]
    for load in loads:
        load.start()

    barrier = pltpu.get_barrier_semaphore()
    for o in range(1, nr):
        pl.semaphore_signal(
            barrier, inc=1, device_id={"rows": lax.rem(r + o, nr)}, device_id_type=MESH
        )

    @pl.when(c > 0)
    def _():
        pl.semaphore_signal(barrier, inc=1, device_id={"chan": c - 1}, device_id_type=MESH)

    @pl.when(c < nc - 1)
    def _():
        pl.semaphore_signal(barrier, inc=1, device_id={"chan": c + 1}, device_id_type=MESH)

    def moment_copy(conv, o):
        return pltpu.make_async_remote_copy(
            src_ref=mom.at[conv, 0], dst_ref=mom.at[conv, o],
            send_sem=mom_send.at[conv, o], recv_sem=mom_recv.at[conv, o],
            device_id={"rows": lax.rem(r + o, nr)}, device_id_type=MESH,
        )

    def halo_copy(src, conv, kind, side):
        row, step = (band - 1, 1) if side == 0 else (0, nr - 1)
        span = pl.ds(0, past) if kind == 0 else pl.ds(past, frames)
        return pltpu.make_async_remote_copy(
            src_ref=src.at[:, row], dst_ref=halo.at[conv, side, span],
            send_sem=halo_send.at[conv, kind, side], recv_sem=halo_recv.at[conv, kind, side],
            device_id={"rows": lax.rem(r + step, nr)}, device_id_type=MESH,
        )

    def sends_halo(side):
        return r < nr - 1 if side == 0 else r > 0

    def gets_halo(side):
        return r > 0 if side == 0 else r < nr - 1

    def halo_start(src, conv, kind):
        for side in range(2):
            @pl.when(sends_halo(side))
            def _():
                halo_copy(src, conv, kind, side).start()

    def halo_wait(src, conv, kind):
        for side in range(2):
            @pl.when(gets_halo(side))
            def _():
                halo_copy(src, conv, kind, side).wait_recv()

    def halo_drain(src, conv, kind):
        for side in range(2):
            @pl.when(sends_halo(side))
            def _():
                halo_copy(src, conv, kind, side).wait_send()

    def moments(ref, conv):
        v = ref[...].reshape(cells, ch).astype(F32)
        mom[conv, 0] = jnp.concatenate(
            [
                jnp.sum(v, axis=0, keepdims=True),
                jnp.sum(v * v, axis=0, keepdims=True),
                jnp.zeros((6, ch), F32),
            ],
            axis=0,
        )

    def statistics(conv):
        total = mom[conv, 0]
        for o in range(1, nr):
            moment_copy(conv, o).wait_recv()
            total = total + mom[conv, o]
        per_group = channels // GROUPS
        i = lax.broadcasted_iota(jnp.int32, (ch, ch), 0) // per_group
        j = lax.broadcasted_iota(jnp.int32, (ch, ch), 1) // per_group
        same = jnp.where(i == j, 1.0, 0.0).astype(F32)
        total = lax.dot_general(
            total, same, (((1,), (0,)), ((), ())),
            precision=lax.Precision.HIGHEST, preferred_element_type=F32,
        )
        total = total * (1.0 / (per_group * cells * nr))
        average = total[0:1]
        return average, lax.rsqrt(total[1:2] - average * average + 1e-06)

    def place(conv, j, p, v):
        s = lax.broadcasted_iota(jnp.int32, (width, ch), 0)
        low = jnp.where(s == 0, 0.0, pltpu.roll(v, 1, 0))
        high = jnp.where(s == width - 1, 0.0, pltpu.roll(v, width - 1, 0))
        for ds, t in enumerate((low, v, high)):
            t = t.astype(BF16)
            for dr in range(3):
                if 0 <= p - dr < band:
                    first = (dr * 3 + ds) * ch
                    x9[conv, j, p - dr, :, first : first + ch] = t

    def row_of(src, conv, j, f, p):
        if p == 0:
            return halo[conv, 0, j]
        if p == band + 1:
            return halo[conv, 1, j]
        return src[f, p - 1]

    def inside(p, v):
        if p == 0:
            return jnp.where(r > 0, v, jnp.zeros_like(v))
        if p == band + 1:
            return jnp.where(r < nr - 1, v, jnp.zeros_like(v))
        return v

    def place_past(conv):
        def body(f, _):
            for p in range(band + 2):
                v = row_of(cv.at[conv], conv, f, f, p).astype(F32)
                place(conv, f, p, inside(p, v))
            return 0

        lax.fori_loop(0, past, body, 0)

    def place_current(src, conv, gain, shift, stats, keep=None):
        average, inverse = stats
        gain, shift = gain[...], shift[...]

        def body(f, _):
            for p in range(band + 2):
                v = row_of(src, conv, f + past, f, p).astype(F32)
                u = ((v - average) * inverse) * gain + shift
                v = (u / (1.0 + jnp.exp(-u))).astype(BF16)
                if keep is not None and 1 <= p <= band:
                    hid[f, p - 1] = v
                place(conv, f + past, p, inside(p, v.astype(F32)))
            return 0

        lax.fori_loop(0, frames, body, 0)

    gw = max(256, ch)
    ngroups = (nc * ch) // gw
    each = gw // ch
    fb = 2 if frames % 2 == 0 else 1
    mb = fb * band * width

    def multiply(conv, g):
        cols = pl.ds(pl.multiple_of(g * gw, gw), gw)

        def body(m, _):
            acc = None
            for dt in range(3):
                lhs = x9[conv, pl.ds(m * fb + dt, fb)].reshape(mb, taps)
                prod = jnp.dot(
                    lhs, w[conv, dt * taps : (dt + 1) * taps, cols], preferred_element_type=F32
                )
                acc = prod if acc is None else acc + prod
            rows = pl.ds(pl.multiple_of(m * mb, mb), mb)
            for q in range(each):
                part[g * each + q, rows] = acc[:, q * ch : (q + 1) * ch]
            return 0

        lax.fori_loop(0, frames // fb, body, 0)

    def rs_copy(conv, d, way):
        return pltpu.make_async_remote_copy(
            src_ref=snd.at[conv, d], dst_ref=rcv.at[conv, way, d],
            send_sem=rs_send.at[conv, d], recv_sem=rs_recv.at[conv, way, d],
            device_id={"chan": c + 1 - 2 * way}, device_id_type=MESH,
        )

    def first_send(conv, d, way):
        snd[conv, d] = part[d].astype(BF16)
        rs_copy(conv, d, way).start()

    def pass_on(conv, d, way):
        rs_copy(conv, d, way).wait_recv()
        snd[conv, d] = (part[d] + rcv[conv, way, d].astype(F32)).astype(BF16)
        rs_copy(conv, d, way).start()

    def convolve(conv, bias, meanwhile=None):
        start = jnp.where(c < nc // 2, ngroups // 2, 0)
        far = [(d, 0) for d in range(nc - 1, nc // 2 - 1, -1)]
        near = [(d, 0) for d in range(nc // 2 - 1, 0, -1)]
        far_left = [(d, 1) for d in range(nc // 2)]
        near_left = [(d, 1) for d in range(nc // 2, nc - 1)]
        for i in range(ngroups):
            multiply(conv, lax.rem(start + i, ngroups))
            if i == max(ngroups // 2, 1) - 1:
                @pl.when(c == 0)
                def _():
                    for d, way in far:
                        first_send(conv, d, way)

                @pl.when(c == nc - 1)
                def _():
                    for d, way in far_left:
                        first_send(conv, d, way)

        @pl.when(c == 0)
        def _():
            for d, way in near:
                first_send(conv, d, way)

        @pl.when(c == nc - 1)
        def _():
            for d, way in near_left:
                first_send(conv, d, way)

        if meanwhile is not None:
            meanwhile()

        for (d, _), (e, _) in zip(far + near, far_left + near_left):
            @pl.when((c > 0) & (c < d))
            def _():
                pass_on(conv, d, 0)

            @pl.when((c < nc - 1) & (c > e))
            def _():
                pass_on(conv, e, 1)

        for way, condition in ((0, c > 0), (1, c < nc - 1)):
            @pl.when(condition)
            def _():
                rs_copy(conv, c, way).wait_recv()
                part[c] = part[c] + rcv[conv, way, c].astype(F32)

        return (part[c] + bias[...]).astype(BF16).reshape(frames, band, width, ch)

    loads[0].wait()
    moments(xv, 0)
    pl.semaphore_wait(
        barrier, nr - 1 + jnp.where(c > 0, 1, 0) + jnp.where(c < nc - 1, 1, 0)
    )
    for o in range(1, nr):
        moment_copy(0, o).start()
    halo_start(xv, 0, 1)
    loads[1].wait()
    halo_start(cv.at[0], 0, 0)
    loads[3].wait()
    halo_start(cv.at[1], 1, 0)

    halo_wait(cv.at[0], 0, 0)
    place_past(0)
    halo_wait(xv, 0, 1)
    place_current(xv, 0, g1, s1, statistics(0))
    loads[2].wait()

    def early():
        halo_wait(cv.at[1], 1, 0)
        place_past(1)

    halo_drain(xv, 0, 1)
    xv[...] = convolve(0, b1, early)
    moments(xv, 1)
    for o in range(1, nr):
        moment_copy(1, o).start()
    halo_start(xv, 1, 1)
    halo_wait(xv, 1, 1)
    place_current(xv, 1, g2, s2, statistics(1), keep=True)
    next_ref[...] = hid[frames - past : frames]
    loads[4].wait()
    out_ref[...] = convolve(1, b2)

    halo_drain(cv.at[0], 0, 0)
    halo_drain(cv.at[1], 1, 0)
    halo_drain(xv, 1, 1)
    for conv in range(2):
        for o in range(1, nr):
            moment_copy(conv, o).wait_send()
        for d in range(nc):
            @pl.when(c < d)
            def _():
                rs_copy(conv, d, 0).wait_send()

            @pl.when(c > d)
            def _():
                rs_copy(conv, d, 1).wait_send()


def local(nr, nc, frames_in, cache_first, gain_first, shift_first, kernel_first, bias_first,
          cache_second, gain_second, shift_second, kernel_second, bias_second):
    def inner(a):
        return jnp.transpose(a, (1, 2, 3, 0))

    ch, frames, band, width = frames_in.shape
    past = cache_first.shape[1]
    channels = kernel_first.shape[4]
    depth = 27 * ch
    hbm = pl.BlockSpec(memory_space=pl.ANY)
    vmem = pl.BlockSpec(memory_space=pltpu.VMEM)
    cells = frames * band * width
    decoded, kept = pl.pallas_call(
        functools.partial(kernel, nr, nc, channels),
        out_shape=(
            jax.ShapeDtypeStruct((frames, band, width, ch), BF16),
            jax.ShapeDtypeStruct((past, band, width, ch), BF16),
        ),
        in_specs=[hbm, hbm, vmem, vmem, hbm, vmem, hbm, vmem, vmem, hbm, vmem],
        out_specs=(vmem, vmem),
        scratch_shapes=[
            pltpu.VMEM((frames, band, width, ch), BF16),
            pltpu.VMEM((2, past, band, width, ch), BF16),
            pltpu.VMEM((frames, band, width, ch), BF16),
            pltpu.VMEM((2, depth, channels), BF16),
            pltpu.VMEM((2, past + frames, band, width, 9 * ch), BF16),
            pltpu.VMEM((2, 2, past + frames, width, ch), BF16),
            pltpu.VMEM((2, nr, 8, ch), F32),
            pltpu.VMEM((nc, cells, ch), F32),
            pltpu.VMEM((2, nc, cells, ch), BF16),
            pltpu.VMEM((2, 2, nc, cells, ch), BF16),
            pltpu.SemaphoreType.DMA((5,)),
            pltpu.SemaphoreType.DMA((2, nr)),
            pltpu.SemaphoreType.DMA((2, nr)),
            pltpu.SemaphoreType.DMA((2, 2, 2)),
            pltpu.SemaphoreType.DMA((2, 2, 2)),
            pltpu.SemaphoreType.DMA((2, nc)),
            pltpu.SemaphoreType.DMA((2, 2, nc)),
        ],
        compiler_params=pltpu.CompilerParams(
            collective_id=0, has_side_effects=True, vmem_limit_bytes=50 * 1024 * 1024
        ),
        cost_estimate=pl.CostEstimate(
            flops=4 * cells * depth * channels, bytes_accessed=4 * depth * channels, transcendentals=0
        ),
    )(
        inner(frames_in), inner(cache_first), gain_first[None], shift_first[None],
        kernel_first.reshape(depth, channels), bias_first[None],
        inner(cache_second), gain_second[None], shift_second[None],
        kernel_second.reshape(depth, channels), bias_second[None],
    )
    return jnp.transpose(decoded, (3, 0, 1, 2)), jnp.transpose(kept, (3, 0, 1, 2))


def solution(mesh):
    tile = P("chan", None, ("grp", "rows"), None)
    taps = P(None, None, None, "chan", None)
    return jax.shard_map(
        functools.partial(local, mesh.shape["rows"], mesh.shape["chan"]),
        mesh=mesh,
        in_specs=(
            tile, tile, P("chan"), P("chan"), taps, P("chan"),
            tile, P("chan"), P("chan"), taps, P("chan"),
        ),
        out_specs=(tile, tile),
        check_vma=False,
    )
```

```python
import functools

import jax
import jax.numpy as jnp
from jax import lax
from jax.experimental import pallas as pl
from jax.experimental.pallas import tpu as pltpu
from jax.sharding import PartitionSpec as P

GROUPS = 32
MESH = pl.DeviceIdType.MESH
F32 = jnp.float32
BF16 = jnp.bfloat16


def kernel(
    nr, nc, channels,
    x_hbm, c1_hbm, g1_hbm, s1_hbm, k1_hbm, b1_hbm, c2_hbm, g2_hbm, s2_hbm, k2_hbm, b2_hbm,
    out_ref, next_ref,
    xv, cv, vecs, w, x9, halo, mom, part, snd, rcv,
    loc_sem, mom_send, mom_recv, halo_send, halo_recv, rs_send, rs_recv,
):
    frames, band, width, ch = xv.shape
    past = cv.shape[1]
    taps = 9 * ch
    cells = frames * band * width
    r = lax.axis_index("rows")
    c = lax.axis_index("chan")

    loads = [
        pltpu.make_async_copy(src, dst, loc_sem.at[i])
        for i, (src, dst) in enumerate((
            (x_hbm, xv), (c1_hbm, cv.at[0]), (k1_hbm, w.at[0]),
            (c2_hbm, cv.at[1]), (k2_hbm, w.at[1]),
            (g1_hbm, vecs.at[0]), (s1_hbm, vecs.at[1]), (b1_hbm, vecs.at[2]),
            (g2_hbm, vecs.at[3]), (s2_hbm, vecs.at[4]), (b2_hbm, vecs.at[5]),
        ))
    ]
    for load in loads:
        load.start()

    barrier = pltpu.get_barrier_semaphore()
    for o in range(1, nr):
        pl.semaphore_signal(
            barrier, inc=1, device_id={"rows": lax.rem(r + o, nr)}, device_id_type=MESH
        )

    @pl.when(c > 0)
    def _():
        pl.semaphore_signal(barrier, inc=1, device_id={"chan": c - 1}, device_id_type=MESH)

    @pl.when(c < nc - 1)
    def _():
        pl.semaphore_signal(barrier, inc=1, device_id={"chan": c + 1}, device_id_type=MESH)

    def moment_copy(conv, o):
        return pltpu.make_async_remote_copy(
            src_ref=mom.at[conv, 0], dst_ref=mom.at[conv, o],
            send_sem=mom_send.at[conv, o], recv_sem=mom_recv.at[conv, o],
            device_id={"rows": lax.rem(r + o, nr)}, device_id_type=MESH,
        )

    def halo_copy(src, conv, kind, side):
        row, step = (band - 1, 1) if side == 0 else (0, nr - 1)
        span = pl.ds(0, past) if kind == 0 else pl.ds(past, frames)
        return pltpu.make_async_remote_copy(
            src_ref=src.at[:, row], dst_ref=halo.at[conv, side, span],
            send_sem=halo_send.at[conv, kind, side], recv_sem=halo_recv.at[conv, kind, side],
            device_id={"rows": lax.rem(r + step, nr)}, device_id_type=MESH,
        )

    def sends_halo(side):
        return r < nr - 1 if side == 0 else r > 0

    def gets_halo(side):
        return r > 0 if side == 0 else r < nr - 1

    def halo_start(src, conv, kind):
        for side in range(2):
            @pl.when(sends_halo(side))
            def _():
                halo_copy(src, conv, kind, side).start()

    def halo_wait(src, conv, kind):
        for side in range(2):
            @pl.when(gets_halo(side))
            def _():
                halo_copy(src, conv, kind, side).wait_recv()

    def halo_drain(src, conv, kind):
        for side in range(2):
            @pl.when(sends_halo(side))
            def _():
                halo_copy(src, conv, kind, side).wait_send()

    def sums_of(v):
        v = v.astype(F32)
        return jnp.sum(v, axis=0, keepdims=True), jnp.sum(v * v, axis=0, keepdims=True)

    def set_moments(conv, sums):
        mom[conv, 0] = jnp.concatenate([*sums, jnp.zeros((6, ch), F32)], axis=0)

    def statistics(conv):
        total = mom[conv, 0]
        for o in range(1, nr):
            moment_copy(conv, o).wait_recv()
            total = total + mom[conv, o]
        per_group = channels // GROUPS
        i = lax.broadcasted_iota(jnp.int32, (ch, ch), 0) // per_group
        j = lax.broadcasted_iota(jnp.int32, (ch, ch), 1) // per_group
        same = jnp.where(i == j, 1.0, 0.0).astype(BF16)
        high = total.astype(BF16)
        rest = total - high.astype(F32)
        middle = rest.astype(BF16)
        low = (rest - middle.astype(F32)).astype(BF16)
        thirds = jnp.concatenate([t.astype(F32) for t in (high, middle, low)], axis=0)
        thirds = jnp.dot(thirds.astype(BF16), same, preferred_element_type=F32)
        total = (thirds[16:24] + thirds[8:16]) + thirds[0:8]
        total = total * (1.0 / (per_group * cells * nr))
        average = total[0:1]
        return average, lax.rsqrt(total[1:2] - average * average + 1e-06)

    def place(conv, j, p, v):
        s = lax.broadcasted_iota(jnp.int32, (width, ch), 0)
        low = jnp.where(s == 0, 0.0, pltpu.roll(v, 1, 0))
        high = jnp.where(s == width - 1, 0.0, pltpu.roll(v, width - 1, 0))
        for ds, t in enumerate((low, v, high)):
            t = t.astype(BF16)
            for dr in range(3):
                if 0 <= p - dr < band:
                    first = (dr * 3 + ds) * ch
                    x9[conv, j, p - dr, :, first : first + ch] = t

    def row_of(src, conv, j, f, p):
        if p == 0:
            return halo[conv, 0, j]
        if p == band + 1:
            return halo[conv, 1, j]
        return src[f, p - 1]

    def inside(p, v):
        if p == 0:
            return jnp.where(r > 0, v, jnp.zeros_like(v))
        if p == band + 1:
            return jnp.where(r < nr - 1, v, jnp.zeros_like(v))
        return v

    def place_past(conv):
        def body(f, _):
            for p in range(band + 2):
                v = row_of(cv.at[conv], conv, f, f, p).astype(F32)
                place(conv, f, p, inside(p, v))
            return 0

        lax.fori_loop(0, past, body, 0)

    def place_current(src, conv, gain, shift, stats, sides, keep=False):
        average, inverse = stats
        gain, shift = vecs[gain], vecs[shift]

        def body(f, _):
            for p in sides:
                v = row_of(src, conv, f + past, f, p).astype(F32)
                u = ((v - average) * inverse) * gain + shift
                v = (u / (1.0 + jnp.exp(-u))).astype(BF16)
                if keep:
                    @pl.when(f >= frames - past)
                    def _():
                        next_ref[f - (frames - past), p - 1] = v
                place(conv, f + past, p, inside(p, v.astype(F32)))
            return 0

        lax.fori_loop(0, frames, body, 0)

    own, edges = range(1, band + 1), (0, band + 1)
    gw = max(256, ch)
    ngroups = (nc * ch) // gw
    each = gw // ch
    fb = 2 if frames % 2 == 0 else 1
    mb = fb * band * width

    piece = band * width

    def multiply(conv, g, m):
        cols = pl.ds(pl.multiple_of(g * gw, gw), gw)
        acc = None
        for dt in range(3):
            lhs = x9[conv, pl.ds(m * fb + dt, fb)].reshape(mb, taps)
            prod = jnp.dot(
                lhs, w[conv, dt * taps : (dt + 1) * taps, cols], preferred_element_type=F32
            )
            acc = prod if acc is None else acc + prod
        rows = pl.ds(pl.multiple_of(m * mb, mb), mb)
        for q in range(each):
            part[g * each + q, rows] = acc[:, q * ch : (q + 1) * ch]

    def rs_copy(conv, d, m, way):
        return pltpu.make_async_remote_copy(
            src_ref=snd.at[conv, d, m], dst_ref=rcv.at[conv, way, d, m],
            send_sem=rs_send.at[conv, d, m], recv_sem=rs_recv.at[conv, way, d, m],
            device_id={"chan": c + 1 - 2 * way}, device_id_type=MESH,
        )

    def rows_of(m):
        return pl.ds(pl.multiple_of(m * piece, piece), piece)

    def first_send(conv, d, way, start, count):
        def body(i, _):
            m = start + i
            snd[conv, d, m] = part[d, rows_of(m)].astype(BF16)
            rs_copy(conv, d, m, way).start()
            return 0

        lax.fori_loop(0, count, body, 0)

    def pass_on(conv, d, way):
        def body(m, _):
            rs_copy(conv, d, m, way).wait_recv()
            total = part[d, rows_of(m)] + rcv[conv, way, d, m].astype(F32)
            snd[conv, d, m] = total.astype(BF16)
            rs_copy(conv, d, m, way).start()
            return 0

        lax.fori_loop(0, frames, body, 0)

    def convolve(conv, bias, dst, meanwhile=None):
        start = jnp.where(c < nc // 2, ngroups // 2, 0)
        half = max(ngroups // 2, 1)
        right = [(d, 0) for d in range(nc - 1, 0, -1)]
        left = [(d, 1) for d in range(nc - 1)]
        blocks = frames // fb

        def steps(first, count):
            def body(i, _):
                g = lax.rem(start + first + i // blocks, ngroups)
                m = lax.rem(i, blocks)
                multiply(conv, g, m)
                if first == 0:
                    @pl.when((c == 0) & (i >= (half - 1) * blocks))
                    def _():
                        first_send(conv, nc - 1, 0, m * fb, fb)

                    @pl.when((c == nc - 1) & (i >= (half - 1) * blocks))
                    def _():
                        first_send(conv, 0, 1, m * fb, fb)
                return 0

            lax.fori_loop(0, count * blocks, body, 0)

        def ends(low, high):
            @pl.when(c == 0)
            def _():
                for d, way in right[low:high]:
                    first_send(conv, d, way, 0, frames)

            @pl.when(c == nc - 1)
            def _():
                for d, way in left[low:high]:
                    first_send(conv, d, way, 0, frames)

        steps(0, half)
        ends(1, nc // 2)
        if ngroups > half:
            steps(half, ngroups - half)
        ends(max(nc // 2, 1), nc - 1)
        if meanwhile is not None:
            meanwhile()

        def relay(near, far):
            for (d, way), (e, yaw) in zip(near, far):
                for chunk, to in ((d, way), (e, yaw)):
                    beyond = (c > 0) & (c < chunk) if to == 0 else (c < nc - 1) & (c > chunk)

                    @pl.when(beyond)
                    def _():
                        pass_on(conv, chunk, to)

        @pl.when(c < nc // 2)
        def _():
            relay(right, left)

        @pl.when(c >= nc // 2)
        def _():
            relay(left, right)

        def body(m, sums):
            for way, condition in ((0, c > 0), (1, c < nc - 1)):
                @pl.when(condition)
                def _():
                    rs_copy(conv, c, m, way).wait_recv()
                    part[c, rows_of(m)] = part[c, rows_of(m)] + rcv[conv, way, c, m].astype(F32)
            v = (part[c, rows_of(m)] + vecs[bias]).astype(BF16)
            dst[m] = v.reshape(band, width, ch)
            more = sums_of(v)
            return sums[0] + more[0], sums[1] + more[1]

        zero = jnp.zeros((1, ch), F32)
        return lax.fori_loop(0, frames, body, (zero, zero))

    loads[0].wait()
    set_moments(0, sums_of(xv[...].reshape(cells, ch)))
    pl.semaphore_wait(
        barrier, nr - 1 + jnp.where(c > 0, 1, 0) + jnp.where(c < nc - 1, 1, 0)
    )
    for o in range(1, nr):
        moment_copy(0, o).start()
    halo_start(xv, 0, 1)
    loads[1].wait()
    halo_start(cv.at[0], 0, 0)
    loads[3].wait()
    halo_start(cv.at[1], 1, 0)

    halo_wait(cv.at[0], 0, 0)
    place_past(0)
    for load in loads[5:]:
        load.wait()
    stats = statistics(0)
    place_current(xv, 0, 0, 1, stats, own)
    halo_wait(xv, 0, 1)
    place_current(xv, 0, 0, 1, stats, edges)
    loads[2].wait()
    halo_drain(xv, 0, 1)

    def early():
        halo_wait(cv.at[1], 1, 0)
        place_past(1)

    set_moments(1, convolve(0, 2, xv, early))
    for o in range(1, nr):
        moment_copy(1, o).start()
    halo_start(xv, 1, 1)
    stats = statistics(1)
    place_current(xv, 1, 3, 4, stats, own, keep=True)
    halo_wait(xv, 1, 1)
    place_current(xv, 1, 3, 4, stats, edges)
    loads[4].wait()
    convolve(1, 5, out_ref)

    halo_drain(cv.at[0], 0, 0)
    halo_drain(cv.at[1], 1, 0)
    halo_drain(xv, 1, 1)
    for conv in range(2):
        for o in range(1, nr):
            moment_copy(conv, o).wait_send()
        for d in range(nc):
            for way, condition in ((0, c < d), (1, c > d)):
                @pl.when(condition)
                def _():
                    def body(m, _):
                        rs_copy(conv, d, m, way).wait_send()
                        return 0

                    lax.fori_loop(0, frames, body, 0)


def local(nr, nc, frames_in, cache_first, gain_first, shift_first, kernel_first, bias_first,
          cache_second, gain_second, shift_second, kernel_second, bias_second):
    def inner(a):
        return jnp.transpose(a, (1, 2, 3, 0))

    ch, frames, band, width = frames_in.shape
    past = cache_first.shape[1]
    channels = kernel_first.shape[4]
    depth = 27 * ch
    hbm = pl.BlockSpec(memory_space=pltpu.HBM)
    vmem = pl.BlockSpec(memory_space=pltpu.VMEM)
    cells = frames * band * width
    decoded, kept = pl.pallas_call(
        functools.partial(kernel, nr, nc, channels),
        out_shape=(
            jax.ShapeDtypeStruct((frames, band, width, ch), BF16),
            jax.ShapeDtypeStruct((past, band, width, ch), BF16),
        ),
        in_specs=[hbm] * 11,
        out_specs=(vmem, vmem),
        scratch_shapes=[
            pltpu.VMEM((frames, band, width, ch), BF16),
            pltpu.VMEM((2, past, band, width, ch), BF16),
            pltpu.VMEM((6, 1, ch), F32),
            pltpu.VMEM((2, depth, channels), BF16),
            pltpu.VMEM((2, past + frames, band, width, 9 * ch), BF16),
            pltpu.VMEM((2, 2, past + frames, width, ch), BF16),
            pltpu.VMEM((2, nr, 8, ch), F32),
            pltpu.VMEM((nc, cells, ch), F32),
            pltpu.VMEM((2, nc, frames, band * width, ch), BF16),
            pltpu.VMEM((2, 2, nc, frames, band * width, ch), BF16),
            pltpu.SemaphoreType.DMA((11,)),
            pltpu.SemaphoreType.DMA((2, nr)),
            pltpu.SemaphoreType.DMA((2, nr)),
            pltpu.SemaphoreType.DMA((2, 2, 2)),
            pltpu.SemaphoreType.DMA((2, 2, 2)),
            pltpu.SemaphoreType.DMA((2, nc, frames)),
            pltpu.SemaphoreType.DMA((2, 2, nc, frames)),
        ],
        compiler_params=pltpu.CompilerParams(
            collective_id=0, has_side_effects=True, vmem_limit_bytes=63 * 1024 * 1024
        ),
        cost_estimate=pl.CostEstimate(
            flops=4 * cells * depth * channels, bytes_accessed=4 * depth * channels, transcendentals=0
        ),
    )(
        inner(frames_in), inner(cache_first), gain_first[None], shift_first[None],
        kernel_first.reshape(depth, channels), bias_first[None],
        inner(cache_second), gain_second[None], shift_second[None],
        kernel_second.reshape(depth, channels), bias_second[None],
    )
    return jnp.transpose(decoded, (3, 0, 1, 2)), jnp.transpose(kept, (3, 0, 1, 2))


def solution(mesh):
    tile = P("chan", None, ("grp", "rows"), None)
    taps = P(None, None, None, "chan", None)
    return jax.shard_map(
        functools.partial(local, mesh.shape["rows"], mesh.shape["chan"]),
        mesh=mesh,
        in_specs=(
            tile, tile, P("chan"), P("chan"), taps, P("chan"),
            tile, P("chan"), P("chan"), taps, P("chan"),
        ),
        out_specs=(tile, tile),
        check_vma=False,
    )
```

```python
import functools

import jax
import jax.numpy as jnp
from jax import lax
from jax.experimental import pallas as pl
from jax.experimental.pallas import tpu as pltpu
from jax.sharding import PartitionSpec as P

GROUPS = 32
MESH = pl.DeviceIdType.MESH
F32 = jnp.float32
BF16 = jnp.bfloat16


def kernel(
    nr, nc, channels,
    x_hbm, c1_hbm, g1_hbm, s1_hbm, k1_hbm, b1_hbm, c2_hbm, g2_hbm, s2_hbm, k2_hbm, b2_hbm,
    out_hbm, next_hbm,
    xv, cv, vecs, kept, w, x9, halo, mom, part, snd, rcv,
    loc_sem, out_sem, mom_send, mom_recv, halo_send, halo_recv, rs_send, rs_recv,
):
    frames, band, width, ch = xv.shape
    past = cv.shape[1]
    taps = 9 * ch
    cells = frames * band * width
    fb = 2 if frames % 2 == 0 else 1
    r = lax.axis_index("rows")
    c = lax.axis_index("chan")

    loads = [
        pltpu.make_async_copy(src, dst, loc_sem.at[i])
        for i, (src, dst) in enumerate((
            (x_hbm, xv), (c1_hbm, cv.at[0]), (k1_hbm, w.at[0]),
            (c2_hbm, cv.at[1]), (k2_hbm, w.at[1]),
            (g1_hbm, vecs.at[0]), (s1_hbm, vecs.at[1]), (b1_hbm, vecs.at[2]),
            (g2_hbm, vecs.at[3]), (s2_hbm, vecs.at[4]), (b2_hbm, vecs.at[5]),
        ))
    ]
    barrier = pltpu.get_barrier_semaphore()
    for o in range(1, nr):
        pl.semaphore_signal(
            barrier, inc=1, device_id={"rows": lax.rem(r + o, nr)}, device_id_type=MESH
        )

    @pl.when(c > 0)
    def _():
        pl.semaphore_signal(barrier, inc=1, device_id={"chan": c - 1}, device_id_type=MESH)

    @pl.when(c < nc - 1)
    def _():
        pl.semaphore_signal(barrier, inc=1, device_id={"chan": c + 1}, device_id_type=MESH)

    for i in (0, 1, 3, *range(5, len(loads))):
        loads[i].start()

    def moment_copy(conv, o):
        return pltpu.make_async_remote_copy(
            src_ref=mom.at[conv, 0], dst_ref=mom.at[conv, o],
            send_sem=mom_send.at[conv, o], recv_sem=mom_recv.at[conv, o],
            device_id={"rows": lax.rem(r + o, nr)}, device_id_type=MESH,
        )

    def halo_copy(src, conv, kind, side):
        row, step = (band - 1, 1) if side == 0 else (0, nr - 1)
        span = pl.ds(0, past) if kind == 0 else pl.ds(past, frames)
        return pltpu.make_async_remote_copy(
            src_ref=src.at[:, row], dst_ref=halo.at[conv, side, span],
            send_sem=halo_send.at[conv, kind, side], recv_sem=halo_recv.at[conv, kind, side],
            device_id={"rows": lax.rem(r + step, nr)}, device_id_type=MESH,
        )

    def sends_halo(side):
        return r < nr - 1 if side == 0 else r > 0

    def gets_halo(side):
        return r > 0 if side == 0 else r < nr - 1

    def halo_start(src, conv, kind):
        for side in range(2):
            @pl.when(sends_halo(side))
            def _():
                halo_copy(src, conv, kind, side).start()

    def halo_wait(src, conv, kind):
        for side in range(2):
            @pl.when(gets_halo(side))
            def _():
                halo_copy(src, conv, kind, side).wait_recv()

    def halo_drain(src, conv, kind):
        for side in range(2):
            @pl.when(sends_halo(side))
            def _():
                halo_copy(src, conv, kind, side).wait_send()

    def sums_of(v):
        v = v.astype(F32)
        return jnp.sum(v, axis=0, keepdims=True), jnp.sum(v * v, axis=0, keepdims=True)

    def set_moments(conv, sums):
        mom[conv, 0] = jnp.concatenate([*sums, jnp.zeros((6, ch), F32)], axis=0)

    def statistics(conv):
        total = mom[conv, 0]
        for o in range(1, nr):
            moment_copy(conv, o).wait_recv()
            total = total + mom[conv, o]
        per_group = channels // GROUPS
        i = lax.broadcasted_iota(jnp.int32, (ch, ch), 0) // per_group
        j = lax.broadcasted_iota(jnp.int32, (ch, ch), 1) // per_group
        same = jnp.where(i == j, 1.0, 0.0).astype(BF16)
        high = total.astype(BF16)
        rest = total - high.astype(F32)
        middle = rest.astype(BF16)
        low = (rest - middle.astype(F32)).astype(BF16)
        thirds = jnp.concatenate([t.astype(F32) for t in (high, middle, low)], axis=0)
        thirds = jnp.dot(thirds.astype(BF16), same, preferred_element_type=F32)
        total = (thirds[16:24] + thirds[8:16]) + thirds[0:8]
        total = total * (1.0 / (per_group * cells * nr))
        average = total[0:1]
        return average, lax.rsqrt(total[1:2] - average * average + 1e-06)

    def place(conv, j, p, v):
        s = lax.broadcasted_iota(jnp.int32, (width, ch), 0)
        low = jnp.where(s == 0, 0.0, pltpu.roll(v, 1, 0))
        high = jnp.where(s == width - 1, 0.0, pltpu.roll(v, width - 1, 0))
        for ds, t in enumerate((low, v, high)):
            t = t.astype(BF16)
            for dr in range(3):
                if 0 <= p - dr < band:
                    first = (dr * 3 + ds) * ch
                    x9[conv, j, p - dr, :, first : first + ch] = t

    def row_of(src, conv, j, f, p):
        if p == 0:
            return halo[conv, 0, j]
        if p == band + 1:
            return halo[conv, 1, j]
        return src[f, p - 1]

    def inside(p, v):
        if p == 0:
            return jnp.where(r > 0, v, jnp.zeros_like(v))
        if p == band + 1:
            return jnp.where(r < nr - 1, v, jnp.zeros_like(v))
        return v

    def place_past(conv):
        def body(f, _):
            for p in range(band + 2):
                v = row_of(cv.at[conv], conv, f, f, p).astype(F32)
                place(conv, f, p, inside(p, v))
            return 0

        lax.fori_loop(0, past, body, 0)

    def place_current(src, conv, gain, shift, stats, sides, first, keep=False):
        average, inverse = stats
        gain, shift = vecs[gain], vecs[shift]

        def body(f, _):
            for p in sides:
                v = row_of(src, conv, f + past, f, p).astype(F32)
                u = ((v - average) * inverse) * gain + shift
                v = (u / (1.0 + jnp.exp(-u))).astype(BF16)
                if keep:
                    @pl.when(f >= frames - past)
                    def _():
                        kept[f - (frames - past), p - 1] = v
                place(conv, f + past, p, inside(p, v.astype(F32)))
            return 0

        lax.fori_loop(first, first + fb, body, 0)

    own, edges = range(1, band + 1), (0, band + 1)
    gw = max(256, ch)
    ngroups = (nc * ch) // gw
    each = gw // ch
    mb = fb * band * width

    piece = band * width

    def multiply(conv, g, m):
        cols = pl.ds(pl.multiple_of(g * gw, gw), gw)
        acc = None
        for dt in range(3):
            lhs = x9[conv, pl.ds(m * fb + dt, fb)].reshape(mb, taps)
            prod = jnp.dot(
                lhs, w[conv, dt * taps : (dt + 1) * taps, cols], preferred_element_type=F32
            )
            acc = prod if acc is None else acc + prod
        rows = pl.ds(pl.multiple_of(m * mb, mb), mb)
        for q in range(each):
            part[g * each + q, rows] = acc[:, q * ch : (q + 1) * ch]

    def rs_copy(conv, d, m, way):
        return pltpu.make_async_remote_copy(
            src_ref=snd.at[conv, d, m], dst_ref=rcv.at[conv, way, d, m],
            send_sem=rs_send.at[conv, d, m], recv_sem=rs_recv.at[conv, way, d, m],
            device_id={"chan": c + 1 - 2 * way}, device_id_type=MESH,
        )

    def rows_of(m):
        return pl.ds(pl.multiple_of(m * piece, piece), piece)

    def first_send(conv, d, way, start, count):
        def body(i, _):
            m = start + i
            snd[conv, d, m] = part[d, rows_of(m)].astype(BF16)
            rs_copy(conv, d, m, way).start()
            return 0

        lax.fori_loop(0, count, body, 0)

    def pass_on(conv, d, way):
        def body(m, _):
            rs_copy(conv, d, m, way).wait_recv()
            total = part[d, rows_of(m)] + rcv[conv, way, d, m].astype(F32)
            snd[conv, d, m] = total.astype(BF16)
            rs_copy(conv, d, m, way).start()
            return 0

        lax.fori_loop(0, frames, body, 0)

    def convolve(conv, bias, prepare, finish, meanwhile=None):
        start = jnp.where(c < nc // 2, ngroups // 2, 0)
        half = max(ngroups // 2, 1)
        right = [(d, 0) for d in range(nc - 1, 0, -1)]
        left = [(d, 1) for d in range(nc - 1)]
        blocks = frames // fb

        def ends(low, high):
            @pl.when(c == 0)
            def _():
                for d, way in right[low:high]:
                    first_send(conv, d, way, 0, frames)

            @pl.when(c == nc - 1)
            def _():
                for d, way in left[low:high]:
                    first_send(conv, d, way, 0, frames)

        def steps(first, count):
            def body(i, _):
                g = lax.rem(start + first + i // blocks, ngroups)
                m = lax.rem(i, blocks)
                if first == 0:
                    if half == 1:
                        prepare(m)
                    else:
                        pl.when(i < blocks)(lambda: prepare(m))
                multiply(conv, g, m)
                if first == 0:
                    @pl.when((c == 0) & (i >= (half - 1) * blocks))
                    def _():
                        first_send(conv, nc - 1, 0, m * fb, fb)

                    @pl.when((c == nc - 1) & (i >= (half - 1) * blocks))
                    def _():
                        first_send(conv, 0, 1, m * fb, fb)
                else:
                    pl.when(i == 0)(lambda: ends(1, nc // 2))
                return 0

            lax.fori_loop(0, count * blocks, body, 0)

        steps(0, half)
        if ngroups > half:
            steps(half, ngroups - half)
        else:
            ends(1, nc // 2)
        ends(max(nc // 2, 1), nc - 1)
        if meanwhile is not None:
            meanwhile()

        def relay(near, far):
            for (d, way), (e, yaw) in zip(near, far):
                for chunk, to in ((d, way), (e, yaw)):
                    beyond = (c > 0) & (c < chunk) if to == 0 else (c < nc - 1) & (c > chunk)

                    @pl.when(beyond)
                    def _():
                        pass_on(conv, chunk, to)

        @pl.when(c < nc // 2)
        def _():
            relay(right, left)

        @pl.when(c >= nc // 2)
        def _():
            relay(left, right)

        def body(m, sums):
            for way, condition in ((0, c > 0), (1, c < nc - 1)):
                @pl.when(condition)
                def _():
                    rs_copy(conv, c, m, way).wait_recv()
                    part[c, rows_of(m)] = part[c, rows_of(m)] + rcv[conv, way, c, m].astype(F32)
            v = (part[c, rows_of(m)] + vecs[bias]).astype(BF16)
            xv[m] = v.reshape(band, width, ch)
            finish(m)
            more = sums_of(v)
            return sums[0] + more[0], sums[1] + more[1]

        zero = jnp.zeros((1, ch), F32)
        return lax.fori_loop(0, frames, body, (zero, zero))

    def prepare(conv, gain, shift, stats, keep):
        def body(m):
            @pl.when(m > 0)
            def _():
                place_current(xv, conv, gain, shift, stats, own, m * fb, keep)

            place_current(xv, conv, gain, shift, stats, edges, m * fb)

        place_current(xv, conv, gain, shift, stats, own, 0, keep)
        halo_wait(xv, conv, 1)
        return body

    def out_copy(f):
        return pltpu.make_async_copy(xv.at[f], out_hbm.at[f], out_sem.at[f])

    next_copy = pltpu.make_async_copy(kept, next_hbm, out_sem.at[frames])

    loads[0].wait()
    loads[2].start()
    set_moments(0, sums_of(xv[...].reshape(cells, ch)))
    pl.semaphore_wait(
        barrier, nr - 1 + jnp.where(c > 0, 1, 0) + jnp.where(c < nc - 1, 1, 0)
    )
    for o in range(1, nr):
        moment_copy(0, o).start()
    halo_start(xv, 0, 1)
    loads[1].wait()
    halo_start(cv.at[0], 0, 0)
    loads[3].wait()
    halo_start(cv.at[1], 1, 0)
    loads[4].start()

    halo_wait(cv.at[0], 0, 0)
    place_past(0)
    for load in loads[5:]:
        load.wait()
    ready = prepare(0, 0, 1, statistics(0), False)
    loads[2].wait()

    def early():
        halo_wait(cv.at[1], 1, 0)
        place_past(1)
        halo_drain(xv, 0, 1)

    set_moments(1, convolve(0, 2, ready, lambda m: None, early))
    for o in range(1, nr):
        moment_copy(1, o).start()
    halo_start(xv, 1, 1)
    ready = prepare(1, 3, 4, statistics(1), True)
    loads[4].wait()

    def saved():
        next_copy.start()
        halo_drain(xv, 1, 1)

    convolve(1, 5, ready, lambda m: out_copy(m).start(), saved)
    for f in range(frames):
        out_copy(f).wait()
    next_copy.wait()

    halo_drain(cv.at[0], 0, 0)
    halo_drain(cv.at[1], 1, 0)
    for conv in range(2):
        for o in range(1, nr):
            moment_copy(conv, o).wait_send()
        for d in range(nc):
            for way, condition in ((0, c < d), (1, c > d)):
                @pl.when(condition)
                def _():
                    def body(m, _):
                        rs_copy(conv, d, m, way).wait_send()
                        return 0

                    lax.fori_loop(0, frames, body, 0)


def hand_over(a_hbm, b_hbm, c_hbm, d_hbm, sems):
    copies = []
    for src, dst in ((a_hbm, c_hbm), (b_hbm, d_hbm)):
        for f in range(src.shape[0]):
            copies.append(pltpu.make_async_copy(src.at[f], dst.at[f], sems.at[len(copies)]))
    for copy in copies:
        copy.start()
    for copy in copies:
        copy.wait()


def local(nr, nc, frames_in, cache_first, gain_first, shift_first, kernel_first, bias_first,
          cache_second, gain_second, shift_second, kernel_second, bias_second):
    def inner(a):
        return jnp.transpose(a, (1, 2, 3, 0))

    ch, frames, band, width = frames_in.shape
    past = cache_first.shape[1]
    channels = kernel_first.shape[4]
    depth = 27 * ch
    hbm = pl.BlockSpec(memory_space=pltpu.HBM)
    cells = frames * band * width
    decoded, kept = pl.pallas_call(
        functools.partial(kernel, nr, nc, channels),
        out_shape=(
            jax.ShapeDtypeStruct((frames, band, width, ch), BF16),
            jax.ShapeDtypeStruct((past, band, width, ch), BF16),
        ),
        in_specs=[hbm] * 11,
        out_specs=(hbm, hbm),
        scratch_shapes=[
            pltpu.VMEM((frames, band, width, ch), BF16),
            pltpu.VMEM((2, past, band, width, ch), BF16),
            pltpu.VMEM((6, 1, ch), F32),
            pltpu.VMEM((past, band, width, ch), BF16),
            pltpu.VMEM((2, depth, channels), BF16),
            pltpu.VMEM((2, past + frames, band, width, 9 * ch), BF16),
            pltpu.VMEM((2, 2, past + frames, width, ch), BF16),
            pltpu.VMEM((2, nr, 8, ch), F32),
            pltpu.VMEM((nc, cells, ch), F32),
            pltpu.VMEM((2, nc, frames, band * width, ch), BF16),
            pltpu.VMEM((2, 2, nc, frames, band * width, ch), BF16),
            pltpu.SemaphoreType.DMA((11,)),
            pltpu.SemaphoreType.DMA((frames + 1,)),
            pltpu.SemaphoreType.DMA((2, nr)),
            pltpu.SemaphoreType.DMA((2, nr)),
            pltpu.SemaphoreType.DMA((2, 2, 2)),
            pltpu.SemaphoreType.DMA((2, 2, 2)),
            pltpu.SemaphoreType.DMA((2, nc, frames)),
            pltpu.SemaphoreType.DMA((2, 2, nc, frames)),
        ],
        compiler_params=pltpu.CompilerParams(
            collective_id=0, has_side_effects=True, vmem_limit_bytes=63 * 1024 * 1024
        ),
        cost_estimate=pl.CostEstimate(
            flops=4 * cells * depth * channels, bytes_accessed=4 * depth * channels, transcendentals=0
        ),
    )(
        inner(frames_in), inner(cache_first), gain_first[None], shift_first[None],
        kernel_first.reshape(depth, channels), bias_first[None],
        inner(cache_second), gain_second[None], shift_second[None],
        kernel_second.reshape(depth, channels), bias_second[None],
    )
    decoded, kept = pl.pallas_call(
        hand_over,
        out_shape=(
            jax.ShapeDtypeStruct(decoded.shape, BF16), jax.ShapeDtypeStruct(kept.shape, BF16),
        ),
        in_specs=[hbm, hbm],
        out_specs=(hbm, hbm),
        scratch_shapes=[pltpu.SemaphoreType.DMA((frames + past,))],
        compiler_params=pltpu.CompilerParams(vmem_limit_bytes=63 * 1024 * 1024),
    )(decoded, kept)
    return jnp.transpose(decoded, (3, 0, 1, 2)), jnp.transpose(kept, (3, 0, 1, 2))


def solution(mesh):
    tile = P("chan", None, ("grp", "rows"), None)
    taps = P(None, None, None, "chan", None)
    return jax.shard_map(
        functools.partial(local, mesh.shape["rows"], mesh.shape["chan"]),
        mesh=mesh,
        in_specs=(
            tile, tile, P("chan"), P("chan"), taps, P("chan"),
            tile, P("chan"), P("chan"), taps, P("chan"),
        ),
        out_specs=(tile, tile),
        check_vma=False,
    )
```

```python
import functools

import jax
import jax.numpy as jnp
from jax import lax
from jax.experimental import pallas as pl
from jax.experimental.pallas import tpu as pltpu
from jax.sharding import PartitionSpec as P

GROUPS = 32
MESH = pl.DeviceIdType.MESH
F32 = jnp.float32
BF16 = jnp.bfloat16


def kernel(
    nr, nc, channels,
    x_hbm, c1_hbm, g1_hbm, s1_hbm, k1_hbm, b1_hbm, c2_hbm, g2_hbm, s2_hbm, k2_hbm, b2_hbm,
    out_hbm, next_hbm,
    xv, cv, vecs, kept, w, x9, halo, mom, part, snd, rcv,
    loc_sem, out_sem, mom_send, mom_recv, halo_send, halo_recv, rs_send, rs_recv,
):
    frames, band, width, ch = xv.shape
    past = cv.shape[1]
    taps = 9 * ch
    cells = frames * band * width
    fb = 2 if frames % 2 == 0 else 1
    r = lax.axis_index("rows")
    c = lax.axis_index("chan")

    loads = [
        pltpu.make_async_copy(src, dst, loc_sem.at[i])
        for i, (src, dst) in enumerate((
            (x_hbm, xv), (c1_hbm, cv.at[0]), (k1_hbm, w.at[0]),
            (c2_hbm, cv.at[1]), (k2_hbm, w.at[1]),
            (g1_hbm, vecs.at[0]), (s1_hbm, vecs.at[1]), (b1_hbm, vecs.at[2]),
            (g2_hbm, vecs.at[3]), (s2_hbm, vecs.at[4]), (b2_hbm, vecs.at[5]),
        ))
    ]
    barrier = pltpu.get_barrier_semaphore()
    for o in range(1, nr):
        pl.semaphore_signal(
            barrier, inc=1, device_id={"rows": lax.rem(r + o, nr)}, device_id_type=MESH
        )

    @pl.when(c > 0)
    def _():
        pl.semaphore_signal(barrier, inc=1, device_id={"chan": c - 1}, device_id_type=MESH)

    @pl.when(c < nc - 1)
    def _():
        pl.semaphore_signal(barrier, inc=1, device_id={"chan": c + 1}, device_id_type=MESH)

    for i in (0, 1, 3, *range(5, len(loads))):
        loads[i].start()

    def moment_copy(conv, o):
        return pltpu.make_async_remote_copy(
            src_ref=mom.at[conv, 0], dst_ref=mom.at[conv, o],
            send_sem=mom_send.at[conv, o], recv_sem=mom_recv.at[conv, o],
            device_id={"rows": lax.rem(r + o, nr)}, device_id_type=MESH,
        )

    def halo_copy(src, conv, kind, side):
        row, step = (band - 1, 1) if side == 0 else (0, nr - 1)
        span = pl.ds(0, past) if kind == 0 else pl.ds(past, frames)
        return pltpu.make_async_remote_copy(
            src_ref=src.at[:, row], dst_ref=halo.at[conv, side, span],
            send_sem=halo_send.at[conv, kind, side], recv_sem=halo_recv.at[conv, kind, side],
            device_id={"rows": lax.rem(r + step, nr)}, device_id_type=MESH,
        )

    def sends_halo(side):
        return r < nr - 1 if side == 0 else r > 0

    def gets_halo(side):
        return r > 0 if side == 0 else r < nr - 1

    def halo_start(src, conv, kind):
        for side in range(2):
            @pl.when(sends_halo(side))
            def _():
                halo_copy(src, conv, kind, side).start()

    def halo_wait(src, conv, kind):
        for side in range(2):
            @pl.when(gets_halo(side))
            def _():
                halo_copy(src, conv, kind, side).wait_recv()

    def halo_drain(src, conv, kind):
        for side in range(2):
            @pl.when(sends_halo(side))
            def _():
                halo_copy(src, conv, kind, side).wait_send()

    def sums_of(v):
        v = v.astype(F32)
        return jnp.sum(v, axis=0, keepdims=True), jnp.sum(v * v, axis=0, keepdims=True)

    def set_moments(conv, sums):
        mom[conv, 0] = jnp.concatenate([*sums, jnp.zeros((6, ch), F32)], axis=0)

    def statistics(conv):
        total = mom[conv, 0]
        for o in range(1, nr):
            moment_copy(conv, o).wait_recv()
            total = total + mom[conv, o]
        per_group = channels // GROUPS
        i = lax.broadcasted_iota(jnp.int32, (ch, ch), 0) // per_group
        j = lax.broadcasted_iota(jnp.int32, (ch, ch), 1) // per_group
        same = jnp.where(i == j, 1.0, 0.0).astype(BF16)
        high = total.astype(BF16)
        rest = total - high.astype(F32)
        middle = rest.astype(BF16)
        low = (rest - middle.astype(F32)).astype(BF16)
        thirds = jnp.concatenate([t.astype(F32) for t in (high, middle, low)], axis=0)
        thirds = jnp.dot(thirds.astype(BF16), same, preferred_element_type=F32)
        total = (thirds[16:24] + thirds[8:16]) + thirds[0:8]
        total = total * (1.0 / (per_group * cells * nr))
        average = total[0:1]
        return average, lax.rsqrt(total[1:2] - average * average + 1e-06)

    def place(conv, j, p, v):
        s = lax.broadcasted_iota(jnp.int32, (width, ch), 0)
        low = jnp.where(s == 0, 0.0, pltpu.roll(v, 1, 0))
        high = jnp.where(s == width - 1, 0.0, pltpu.roll(v, width - 1, 0))
        for ds, t in enumerate((low, v, high)):
            t = t.astype(BF16)
            for dr in range(3):
                if 0 <= p - dr < band:
                    first = (dr * 3 + ds) * ch
                    x9[conv, j, p - dr, :, first : first + ch] = t

    def row_of(src, conv, j, f, p):
        if p == 0:
            return halo[conv, 0, j]
        if p == band + 1:
            return halo[conv, 1, j]
        return src[f, p - 1]

    def inside(p, v):
        if p == 0:
            return jnp.where(r > 0, v, jnp.zeros_like(v))
        if p == band + 1:
            return jnp.where(r < nr - 1, v, jnp.zeros_like(v))
        return v

    def place_past(conv, sides):
        def body(f, _):
            for p in sides:
                v = row_of(cv.at[conv], conv, f, f, p).astype(F32)
                place(conv, f, p, inside(p, v))
            return 0

        lax.fori_loop(0, past, body, 0)

    def place_current(src, conv, gain, shift, stats, sides, first, keep=False):
        average, inverse = stats
        gain, shift = vecs[gain], vecs[shift]

        def body(f, _):
            for p in sides:
                v = row_of(src, conv, f + past, f, p).astype(F32)
                u = ((v - average) * inverse) * gain + shift
                v = (u / (1.0 + jnp.exp(-u))).astype(BF16)
                if keep:
                    @pl.when(f >= frames - past)
                    def _():
                        kept[f - (frames - past), p - 1] = v
                place(conv, f + past, p, inside(p, v.astype(F32)))
            return 0

        lax.fori_loop(first, first + fb, body, 0)

    own, edges = range(1, band + 1), (0, band + 1)
    gw = max(256, ch)
    ngroups = (nc * ch) // gw
    each = gw // ch
    mb = fb * band * width

    piece = band * width

    def multiply(conv, g, m):
        cols = pl.ds(pl.multiple_of(g * gw, gw), gw)
        acc = None
        for dt in range(3):
            lhs = x9[conv, pl.ds(m * fb + dt, fb)].reshape(mb, taps)
            prod = jnp.dot(
                lhs, w[conv, dt * taps : (dt + 1) * taps, cols], preferred_element_type=F32
            )
            acc = prod if acc is None else acc + prod
        rows = pl.ds(pl.multiple_of(m * mb, mb), mb)
        for q in range(each):
            part[g * each + q, rows] = acc[:, q * ch : (q + 1) * ch]

    def rs_copy(conv, d, m, way):
        return pltpu.make_async_remote_copy(
            src_ref=snd.at[conv, d, m], dst_ref=rcv.at[conv, way, d, m],
            send_sem=rs_send.at[conv, d, m], recv_sem=rs_recv.at[conv, way, d, m],
            device_id={"chan": c + 1 - 2 * way}, device_id_type=MESH,
        )

    def rows_of(m):
        return pl.ds(pl.multiple_of(m * piece, piece), piece)

    def first_send(conv, d, way, start, count):
        def body(i, _):
            m = start + i
            snd[conv, d, m] = part[d, rows_of(m)].astype(BF16)
            rs_copy(conv, d, m, way).start()
            return 0

        lax.fori_loop(0, count, body, 0)

    def pass_on(conv, d, way, start, count):
        def body(i, _):
            m = start + i
            rs_copy(conv, d, m, way).wait_recv()
            total = part[d, rows_of(m)] + rcv[conv, way, d, m].astype(F32)
            snd[conv, d, m] = total.astype(BF16)
            rs_copy(conv, d, m, way).start()
            return 0

        lax.fori_loop(0, count, body, 0)

    def convolve(conv, bias, prepare, finish, meanwhile):
        start = jnp.where(c < nc // 2, ngroups // 2, 0)
        half = max(ngroups // 2, 1)
        right = [(d, 0) for d in range(nc - 1, 0, -1)]
        left = [(d, 1) for d in range(nc - 1)]
        blocks = frames // fb

        def ends(low, high):
            @pl.when(c == 0)
            def _():
                for d, way in right[low:high]:
                    first_send(conv, d, way, 0, frames)

            @pl.when(c == nc - 1)
            def _():
                for d, way in left[low:high]:
                    first_send(conv, d, way, 0, frames)

        def steps(first, count):
            def body(i, _):
                g = lax.rem(start + first + i // blocks, ngroups)
                m = lax.rem(i, blocks)
                if first == 0:
                    if half == 1:
                        prepare(m)
                    else:
                        pl.when(i < blocks)(lambda: prepare(m))
                multiply(conv, g, m)
                if first == 0:
                    @pl.when((c == 0) & (i >= (half - 1) * blocks))
                    def _():
                        first_send(conv, nc - 1, 0, m * fb, fb)

                    @pl.when((c == nc - 1) & (i >= (half - 1) * blocks))
                    def _():
                        first_send(conv, 0, 1, m * fb, fb)
                else:
                    pl.when(i == 0)(lambda: ends(1, nc // 2))

                    @pl.when((i < blocks) & (c > 0) & (c < nc // 2))
                    def _():
                        pass_on(conv, nc - 1, 0, i * fb, fb)

                    @pl.when((i < blocks) & (c >= nc // 2) & (c < nc - 1))
                    def _():
                        pass_on(conv, 0, 1, i * fb, fb)
                return 0

            lax.fori_loop(0, count * blocks, body, 0)

        steps(0, half)
        if ngroups > half:
            steps(half, ngroups - half)
        else:
            ends(1, nc // 2)
        ends(max(nc // 2, 1), nc - 1)

        def relay(order):
            for d, way in order:
                beyond = (c > 0) & (c < d) if way == 0 else (c < nc - 1) & (c > d)

                @pl.when(beyond)
                def _():
                    pass_on(conv, d, way, 0, frames)

        done = 1 if ngroups > half else 0

        @pl.when(c < nc // 2)
        def _():
            relay(right[:1 - done] + [x for pair in zip(left, right[1:]) for x in pair] + left[-1:])

        @pl.when(c >= nc // 2)
        def _():
            relay(left[:1 - done] + [x for pair in zip(right, left[1:]) for x in pair] + right[-1:])

        meanwhile()

        def body(m, sums):
            for way, condition in ((0, c > 0), (1, c < nc - 1)):
                @pl.when(condition)
                def _():
                    rs_copy(conv, c, m, way).wait_recv()
                    part[c, rows_of(m)] = part[c, rows_of(m)] + rcv[conv, way, c, m].astype(F32)
            v = (part[c, rows_of(m)] + vecs[bias]).astype(BF16)
            xv[m] = v.reshape(band, width, ch)
            finish(m)
            more = sums_of(v)
            return sums[0] + more[0], sums[1] + more[1]

        zero = jnp.zeros((1, ch), F32)
        return lax.fori_loop(0, frames, body, (zero, zero))

    def prepare(conv, gain, shift, stats, keep):
        def body(m):
            @pl.when(m > 0)
            def _():
                place_current(xv, conv, gain, shift, stats, own, m * fb, keep)

            place_current(xv, conv, gain, shift, stats, edges, m * fb)

        place_current(xv, conv, gain, shift, stats, own, 0, keep)
        halo_wait(xv, conv, 1)
        if conv == 0:
            halo_wait(cv.at[0], 0, 0)
            place_past(0, edges)
        return body

    def out_copy(f):
        return pltpu.make_async_copy(xv.at[f], out_hbm.at[f], out_sem.at[f])

    next_copy = pltpu.make_async_copy(kept, next_hbm, out_sem.at[frames])

    loads[0].wait()
    loads[2].start()
    set_moments(0, sums_of(xv[...].reshape(cells, ch)))
    pl.semaphore_wait(
        barrier, nr - 1 + jnp.where(c > 0, 1, 0) + jnp.where(c < nc - 1, 1, 0)
    )
    for o in range(1, nr):
        moment_copy(0, o).start()
    halo_start(xv, 0, 1)
    loads[1].wait()
    halo_start(cv.at[0], 0, 0)
    place_past(0, own)
    for load in loads[5:]:
        load.wait()
    ready = prepare(0, 0, 1, statistics(0), False)
    loads[3].wait()
    halo_start(cv.at[1], 1, 0)
    loads[4].start()
    loads[2].wait()

    def early():
        halo_wait(cv.at[1], 1, 0)
        place_past(1, range(band + 2))
        halo_drain(xv, 0, 1)

    set_moments(1, convolve(0, 2, ready, lambda m: None, early))
    for o in range(1, nr):
        moment_copy(1, o).start()
    halo_start(xv, 1, 1)
    ready = prepare(1, 3, 4, statistics(1), True)
    loads[4].wait()

    def saved():
        next_copy.start()
        halo_drain(xv, 1, 1)

    convolve(1, 5, ready, lambda m: out_copy(m).start(), saved)
    for f in range(frames):
        out_copy(f).wait()
    next_copy.wait()

    halo_drain(cv.at[0], 0, 0)
    halo_drain(cv.at[1], 1, 0)
    for conv in range(2):
        for o in range(1, nr):
            moment_copy(conv, o).wait_send()
        for d in range(nc):
            for way, condition in ((0, c < d), (1, c > d)):
                @pl.when(condition)
                def _():
                    def body(m, _):
                        rs_copy(conv, d, m, way).wait_send()
                        return 0

                    lax.fori_loop(0, frames, body, 0)


def hand_over(a_hbm, b_hbm, c_hbm, d_hbm, a_held, b_held, in_sem, out_sem):
    copies = []
    for src, held, dst in ((a_hbm, a_held, c_hbm), (b_hbm, b_held, d_hbm)):
        for f in range(src.shape[0]):
            i = len(copies)
            copies.append((
                pltpu.make_async_copy(src.at[f], held.at[f], in_sem.at[i]),
                pltpu.make_async_copy(held.at[f], dst.at[f], out_sem.at[i]),
            ))
    for arrive, _ in copies:
        arrive.start()
    for arrive, leave in copies:
        arrive.wait()
        leave.start()
    for _, leave in copies:
        leave.wait()


def local(nr, nc, frames_in, cache_first, gain_first, shift_first, kernel_first, bias_first,
          cache_second, gain_second, shift_second, kernel_second, bias_second):
    def inner(a):
        return jnp.transpose(a, (1, 2, 3, 0))

    ch, frames, band, width = frames_in.shape
    past = cache_first.shape[1]
    channels = kernel_first.shape[4]
    depth = 27 * ch
    hbm = pl.BlockSpec(memory_space=pltpu.HBM)
    cells = frames * band * width
    decoded, kept = pl.pallas_call(
        functools.partial(kernel, nr, nc, channels),
        out_shape=(
            jax.ShapeDtypeStruct((frames, band, width, ch), BF16),
            jax.ShapeDtypeStruct((past, band, width, ch), BF16),
        ),
        in_specs=[hbm] * 11,
        out_specs=(hbm, hbm),
        scratch_shapes=[
            pltpu.VMEM((frames, band, width, ch), BF16),
            pltpu.VMEM((2, past, band, width, ch), BF16),
            pltpu.VMEM((6, 1, ch), F32),
            pltpu.VMEM((past, band, width, ch), BF16),
            pltpu.VMEM((2, depth, channels), BF16),
            pltpu.VMEM((2, past + frames, band, width, 9 * ch), BF16),
            pltpu.VMEM((2, 2, past + frames, width, ch), BF16),
            pltpu.VMEM((2, nr, 8, ch), F32),
            pltpu.VMEM((nc, cells, ch), F32),
            pltpu.VMEM((2, nc, frames, band * width, ch), BF16),
            pltpu.VMEM((2, 2, nc, frames, band * width, ch), BF16),
            pltpu.SemaphoreType.DMA((11,)),
            pltpu.SemaphoreType.DMA((frames + 1,)),
            pltpu.SemaphoreType.DMA((2, nr)),
            pltpu.SemaphoreType.DMA((2, nr)),
            pltpu.SemaphoreType.DMA((2, 2, 2)),
            pltpu.SemaphoreType.DMA((2, 2, 2)),
            pltpu.SemaphoreType.DMA((2, nc, frames)),
            pltpu.SemaphoreType.DMA((2, 2, nc, frames)),
        ],
        compiler_params=pltpu.CompilerParams(
            collective_id=0, has_side_effects=True, vmem_limit_bytes=63 * 1024 * 1024
        ),
        cost_estimate=pl.CostEstimate(
            flops=4 * cells * depth * channels, bytes_accessed=4 * depth * channels, transcendentals=0
        ),
    )(
        inner(frames_in), inner(cache_first), gain_first[None], shift_first[None],
        kernel_first.reshape(depth, channels), bias_first[None],
        inner(cache_second), gain_second[None], shift_second[None],
        kernel_second.reshape(depth, channels), bias_second[None],
    )
    decoded, kept = pl.pallas_call(
        hand_over,
        out_shape=(
            jax.ShapeDtypeStruct(decoded.shape, BF16), jax.ShapeDtypeStruct(kept.shape, BF16),
        ),
        in_specs=[hbm, hbm],
        out_specs=(hbm, hbm),
        scratch_shapes=[
            pltpu.VMEM(decoded.shape, BF16), pltpu.VMEM(kept.shape, BF16),
            pltpu.SemaphoreType.DMA((frames + past,)), pltpu.SemaphoreType.DMA((frames + past,)),
        ],
        compiler_params=pltpu.CompilerParams(vmem_limit_bytes=63 * 1024 * 1024),
    )(decoded, kept)
    return jnp.transpose(decoded, (3, 0, 1, 2)), jnp.transpose(kept, (3, 0, 1, 2))


def solution(mesh):
    tile = P("chan", None, ("grp", "rows"), None)
    taps = P(None, None, None, "chan", None)
    return jax.shard_map(
        functools.partial(local, mesh.shape["rows"], mesh.shape["chan"]),
        mesh=mesh,
        in_specs=(
            tile, tile, P("chan"), P("chan"), taps, P("chan"),
            tile, P("chan"), P("chan"), taps, P("chan"),
        ),
        out_specs=(tile, tile),
        check_vma=False,
    )
```

```python
import functools

import jax
import jax.numpy as jnp
from jax import lax
from jax.experimental import pallas as pl
from jax.experimental.pallas import tpu as pltpu
from jax.sharding import PartitionSpec as P

GROUPS = 32
MESH = pl.DeviceIdType.MESH
F32 = jnp.float32
BF16 = jnp.bfloat16


def kernel(
    nr, nc, channels,
    x_hbm, c1_hbm, g1_hbm, s1_hbm, k1_hbm, b1_hbm, c2_hbm, g2_hbm, s2_hbm, k2_hbm, b2_hbm,
    out_hbm, next_hbm,
    xv, cv, vecs, kept, w, x9, halo, mom, part, snd, rcv,
    loc_sem, out_sem, mom_send, mom_recv, halo_send, halo_recv, rs_send, rs_recv,
):
    frames, band, width, ch = xv.shape
    past = cv.shape[1]
    taps = 9 * ch
    cells = frames * band * width
    fb = 2 if frames % 2 == 0 else 1
    r = lax.axis_index("rows")
    c = lax.axis_index("chan")
    half_line = nc // 2
    side = c // half_line
    inner = 1 - 2 * side
    place_in = c * (1 - side) + (nc - 1 - c) * side
    border = (place_in + 1) // half_line

    def chunk_at(d):
        return d * (1 - side) + (nc - 1 - d) * side


    loads = [
        pltpu.make_async_copy(src, dst, loc_sem.at[i])
        for i, (src, dst) in enumerate((
            (x_hbm, xv), (c1_hbm, cv.at[0]), (k1_hbm, w.at[0]),
            (c2_hbm, cv.at[1]), (k2_hbm, w.at[1]),
            (g1_hbm, vecs.at[0]), (s1_hbm, vecs.at[1]), (b1_hbm, vecs.at[2]),
            (g2_hbm, vecs.at[3]), (s2_hbm, vecs.at[4]), (b2_hbm, vecs.at[5]),
        ))
    ]
    barrier = pltpu.get_barrier_semaphore()
    for o in range(1, nr):
        pl.semaphore_signal(
            barrier, inc=1, device_id={"rows": lax.rem(r + o, nr)}, device_id_type=MESH
        )

    @pl.when(c > 0)
    def _():
        pl.semaphore_signal(barrier, inc=1, device_id={"chan": c - 1}, device_id_type=MESH)

    @pl.when(c < nc - 1)
    def _():
        pl.semaphore_signal(barrier, inc=1, device_id={"chan": c + 1}, device_id_type=MESH)

    @pl.when(border == 0)
    def _():
        pl.semaphore_signal(
            barrier, inc=1, device_id={"chan": chunk_at(half_line)}, device_id_type=MESH
        )

    for d in range(half_line + 1, nc):
        @pl.when(border == 1)
        def _():
            pl.semaphore_signal(
                barrier, inc=1, device_id={"chan": chunk_at(d)}, device_id_type=MESH
            )

    for i in (0, 1, 3, *range(5, len(loads))):
        loads[i].start()

    def moment_copy(conv, o):
        return pltpu.make_async_remote_copy(
            src_ref=mom.at[conv, 0], dst_ref=mom.at[conv, o],
            send_sem=mom_send.at[conv, o], recv_sem=mom_recv.at[conv, o],
            device_id={"rows": lax.rem(r + o, nr)}, device_id_type=MESH,
        )

    def halo_copy(src, conv, kind, side):
        row, step = (band - 1, 1) if side == 0 else (0, nr - 1)
        span = pl.ds(0, past) if kind == 0 else pl.ds(past, frames)
        return pltpu.make_async_remote_copy(
            src_ref=src.at[:, row], dst_ref=halo.at[conv, side, span],
            send_sem=halo_send.at[conv, kind, side], recv_sem=halo_recv.at[conv, kind, side],
            device_id={"rows": lax.rem(r + step, nr)}, device_id_type=MESH,
        )

    def sends_halo(side):
        return r < nr - 1 if side == 0 else r > 0

    def gets_halo(side):
        return r > 0 if side == 0 else r < nr - 1

    def halo_start(src, conv, kind):
        for side in range(2):
            @pl.when(sends_halo(side))
            def _():
                halo_copy(src, conv, kind, side).start()

    def halo_wait(src, conv, kind):
        for side in range(2):
            @pl.when(gets_halo(side))
            def _():
                halo_copy(src, conv, kind, side).wait_recv()

    def halo_drain(src, conv, kind):
        for side in range(2):
            @pl.when(sends_halo(side))
            def _():
                halo_copy(src, conv, kind, side).wait_send()

    def sums_of(v):
        v = v.astype(F32)
        return jnp.sum(v, axis=0, keepdims=True), jnp.sum(v * v, axis=0, keepdims=True)

    def set_moments(conv, sums):
        mom[conv, 0] = jnp.concatenate([*sums, jnp.zeros((6, ch), F32)], axis=0)

    def statistics(conv):
        total = mom[conv, 0]
        for o in range(1, nr):
            moment_copy(conv, o).wait_recv()
            total = total + mom[conv, o]
        per_group = channels // GROUPS
        i = lax.broadcasted_iota(jnp.int32, (ch, ch), 0) // per_group
        j = lax.broadcasted_iota(jnp.int32, (ch, ch), 1) // per_group
        same = jnp.where(i == j, 1.0, 0.0).astype(BF16)
        high = total.astype(BF16)
        rest = total - high.astype(F32)
        middle = rest.astype(BF16)
        low = (rest - middle.astype(F32)).astype(BF16)
        thirds = jnp.concatenate([t.astype(F32) for t in (high, middle, low)], axis=0)
        thirds = jnp.dot(thirds.astype(BF16), same, preferred_element_type=F32)
        total = (thirds[16:24] + thirds[8:16]) + thirds[0:8]
        total = total * (1.0 / (per_group * cells * nr))
        average = total[0:1]
        return average, lax.rsqrt(total[1:2] - average * average + 1e-06)

    def place(conv, j, p, v):
        s = lax.broadcasted_iota(jnp.int32, (width, ch), 0)
        low = jnp.where(s == 0, 0.0, pltpu.roll(v, 1, 0))
        high = jnp.where(s == width - 1, 0.0, pltpu.roll(v, width - 1, 0))
        for ds, t in enumerate((low, v, high)):
            t = t.astype(BF16)
            for dr in range(3):
                if 0 <= p - dr < band:
                    first = (dr * 3 + ds) * ch
                    x9[conv, j, p - dr, :, first : first + ch] = t

    def row_of(src, conv, j, f, p):
        if p == 0:
            return halo[conv, 0, j]
        if p == band + 1:
            return halo[conv, 1, j]
        return src[f, p - 1]

    def inside(p, v):
        if p == 0:
            return jnp.where(r > 0, v, jnp.zeros_like(v))
        if p == band + 1:
            return jnp.where(r < nr - 1, v, jnp.zeros_like(v))
        return v

    def place_past(conv, sides):
        def body(f, _):
            for p in sides:
                v = row_of(cv.at[conv], conv, f, f, p).astype(F32)
                place(conv, f, p, inside(p, v))
            return 0

        lax.fori_loop(0, past, body, 0)

    def place_current(src, conv, gain, shift, stats, sides, first, keep=False):
        average, inverse = stats
        gain, shift = vecs[gain], vecs[shift]

        def body(f, _):
            for p in sides:
                v = row_of(src, conv, f + past, f, p).astype(F32)
                u = ((v - average) * inverse) * gain + shift
                v = (u / (1.0 + jnp.exp(-u))).astype(BF16)
                if keep:
                    @pl.when(f >= frames - past)
                    def _():
                        kept[f - (frames - past), p - 1] = v
                place(conv, f + past, p, inside(p, v.astype(F32)))
            return 0

        lax.fori_loop(first, first + fb, body, 0)

    own, edges = range(1, band + 1), (0, band + 1)
    gw = max(256, ch)
    ngroups = (nc * ch) // gw
    each = gw // ch
    mb = fb * band * width

    piece = band * width

    def multiply(conv, g, m):
        cols = pl.ds(pl.multiple_of(g * gw, gw), gw)
        acc = None
        for dt in range(3):
            lhs = x9[conv, pl.ds(m * fb + dt, fb)].reshape(mb, taps)
            prod = jnp.dot(
                lhs, w[conv, dt * taps : (dt + 1) * taps, cols], preferred_element_type=F32
            )
            acc = prod if acc is None else acc + prod
        rows = pl.ds(pl.multiple_of(m * mb, mb), mb)
        for q in range(each):
            part[g * each + q, rows] = acc[:, q * ch : (q + 1) * ch]

    def rs_copy(conv, d, m, way, target):
        return pltpu.make_async_remote_copy(
            src_ref=snd.at[conv, d, m], dst_ref=rcv.at[conv, way, d, m],
            send_sem=rs_send.at[conv, d, m], recv_sem=rs_recv.at[conv, way, d, m],
            device_id={"chan": target}, device_id_type=MESH,
        )

    def sent_copy(conv, d, m, inward):
        if inward:
            target = border * d + (1 - border) * (c + inner)
            return rs_copy(conv, d, m, 2 * border, target)
        return rs_copy(conv, d, m, 1, c - inner)

    def rows_of(m):
        return pl.ds(pl.multiple_of(m * piece, piece), piece)

    def take(conv, d, m, way):
        rs_copy(conv, d, m, way, lax.rem(c + 1, nc)).wait_recv()
        part[d, rows_of(m)] = part[d, rows_of(m)] + rcv[conv, way, d, m].astype(F32)

    def emit(conv, spot, inward, start, count):
        d = chunk_at(spot)
        way, adds = (0, place_in > 0) if inward else (1, border == 0)

        def body(i, _):
            m = start + i

            @pl.when(adds)
            def _():
                take(conv, d, m, way)

            snd[conv, d, m] = part[d, rows_of(m)].astype(BF16)
            sent_copy(conv, d, m, inward).start()
            return 0

        lax.fori_loop(0, count, body, 0)

    def convolve(conv, bias, prepare, finish, meanwhile):
        start = (1 - side) * (ngroups // 2)
        half = ngroups // 2
        blocks = frames // fb

        def far_block(i, _):
            m = lax.rem(i, blocks)
            pl.when(i < blocks)(lambda: prepare(m))
            multiply(conv, lax.rem(start + i // blocks, ngroups), m)

            @pl.when((place_in == 0) & (i >= (half - 1) * blocks))
            def _():
                emit(conv, nc - 1, True, m * fb, fb)

            return 0

        def near_block(i, _):
            multiply(conv, lax.rem(start + half + i // blocks, ngroups), lax.rem(i, blocks))

            @pl.when((i == 0) & (place_in == 0))
            def _():
                for spot in range(nc - 2, half_line - 1, -1):
                    emit(conv, spot, True, 0, frames)

            @pl.when((i < blocks) & (place_in > 0))
            def _():
                emit(conv, nc - 1, True, i * fb, fb)

            return 0

        lax.fori_loop(0, half * blocks, far_block, 0)
        lax.fori_loop(0, (ngroups - half) * blocks, near_block, 0)

        for spot in range(half_line - 1):
            @pl.when(place_in > spot)
            def _():
                emit(conv, spot, False, 0, frames)

        for spot in range(nc - 2, 0, -1):
            @pl.when((place_in > 0) if spot >= half_line else (place_in < spot))
            def _():
                emit(conv, spot, True, 0, frames)

        meanwhile()

        def body(m, sums):
            for way, condition in ((1, border == 0), (0, place_in > 0)):
                @pl.when(condition)
                def _():
                    take(conv, c, m, way)

            take(conv, c, m, 2)
            v = (part[c, rows_of(m)] + vecs[bias]).astype(BF16)
            xv[m] = v.reshape(band, width, ch)
            finish(m)
            more = sums_of(v)
            return sums[0] + more[0], sums[1] + more[1]

        zero = jnp.zeros((1, ch), F32)
        return lax.fori_loop(0, frames, body, (zero, zero))

    def prepare(conv, gain, shift, stats, keep):
        def body(m):
            @pl.when(m > 0)
            def _():
                place_current(xv, conv, gain, shift, stats, own, m * fb, keep)

            place_current(xv, conv, gain, shift, stats, edges, m * fb)

        place_current(xv, conv, gain, shift, stats, own, 0, keep)
        halo_wait(xv, conv, 1)
        if conv == 0:
            halo_wait(cv.at[0], 0, 0)
            place_past(0, edges)
        return body

    def out_copy(f):
        return pltpu.make_async_copy(xv.at[f], out_hbm.at[f], out_sem.at[f])

    next_copy = pltpu.make_async_copy(kept, next_hbm, out_sem.at[frames])

    loads[0].wait()
    loads[2].start()
    set_moments(0, sums_of(xv[...].reshape(cells, ch)))
    pl.semaphore_wait(
        barrier,
        nr - 1 + jnp.where(c > 0, 1, 0) + jnp.where(c < nc - 1, 1, 0)
        + (1 - border) + border * (nc - half_line - 1),
    )
    for o in range(1, nr):
        moment_copy(0, o).start()
    halo_start(xv, 0, 1)
    loads[1].wait()
    halo_start(cv.at[0], 0, 0)
    place_past(0, own)
    for load in loads[5:]:
        load.wait()
    ready = prepare(0, 0, 1, statistics(0), False)
    loads[3].wait()
    halo_start(cv.at[1], 1, 0)
    loads[4].start()
    loads[2].wait()

    def early():
        halo_wait(cv.at[1], 1, 0)
        place_past(1, range(band + 2))
        halo_drain(xv, 0, 1)

    set_moments(1, convolve(0, 2, ready, lambda m: None, early))
    for o in range(1, nr):
        moment_copy(1, o).start()
    halo_start(xv, 1, 1)
    ready = prepare(1, 3, 4, statistics(1), True)
    loads[4].wait()

    def saved():
        next_copy.start()
        halo_drain(xv, 1, 1)

    convolve(1, 5, ready, lambda m: out_copy(m).start(), saved)
    for f in range(frames):
        out_copy(f).wait()
    next_copy.wait()

    halo_drain(cv.at[0], 0, 0)
    halo_drain(cv.at[1], 1, 0)
    for conv in range(2):
        for o in range(1, nr):
            moment_copy(conv, o).wait_send()
        for d in range(nc):
            @pl.when(c != d)
            def _():
                def body(m, _):
                    rs_copy(conv, d, m, 0, d).wait_send()
                    return 0

                lax.fori_loop(0, frames, body, 0)


def hand_over(a_hbm, b_hbm, c_hbm, d_hbm, a_held, b_held, in_sem, out_sem):
    copies = []
    for src, held, dst in ((a_hbm, a_held, c_hbm), (b_hbm, b_held, d_hbm)):
        for f in range(src.shape[0]):
            i = len(copies)
            copies.append((
                pltpu.make_async_copy(src.at[f], held.at[f], in_sem.at[i]),
                pltpu.make_async_copy(held.at[f], dst.at[f], out_sem.at[i]),
            ))
    for arrive, _ in copies:
        arrive.start()
    for arrive, leave in copies:
        arrive.wait()
        leave.start()
    for _, leave in copies:
        leave.wait()


def local(nr, nc, frames_in, cache_first, gain_first, shift_first, kernel_first, bias_first,
          cache_second, gain_second, shift_second, kernel_second, bias_second):
    def inner(a):
        return jnp.transpose(a, (1, 2, 3, 0))

    ch, frames, band, width = frames_in.shape
    past = cache_first.shape[1]
    channels = kernel_first.shape[4]
    depth = 27 * ch
    hbm = pl.BlockSpec(memory_space=pltpu.HBM)
    cells = frames * band * width
    decoded, kept = pl.pallas_call(
        functools.partial(kernel, nr, nc, channels),
        out_shape=(
            jax.ShapeDtypeStruct((frames, band, width, ch), BF16),
            jax.ShapeDtypeStruct((past, band, width, ch), BF16),
        ),
        in_specs=[hbm] * 11,
        out_specs=(hbm, hbm),
        scratch_shapes=[
            pltpu.VMEM((frames, band, width, ch), BF16),
            pltpu.VMEM((2, past, band, width, ch), BF16),
            pltpu.VMEM((6, 1, ch), F32),
            pltpu.VMEM((past, band, width, ch), BF16),
            pltpu.VMEM((2, depth, channels), BF16),
            pltpu.VMEM((2, past + frames, band, width, 9 * ch), BF16),
            pltpu.VMEM((2, 2, past + frames, width, ch), BF16),
            pltpu.VMEM((2, nr, 8, ch), F32),
            pltpu.VMEM((nc, cells, ch), F32),
            pltpu.VMEM((2, nc, frames, band * width, ch), BF16),
            pltpu.VMEM((2, 3, nc, frames, band * width, ch), BF16),
            pltpu.SemaphoreType.DMA((11,)),
            pltpu.SemaphoreType.DMA((frames + 1,)),
            pltpu.SemaphoreType.DMA((2, nr)),
            pltpu.SemaphoreType.DMA((2, nr)),
            pltpu.SemaphoreType.DMA((2, 2, 2)),
            pltpu.SemaphoreType.DMA((2, 2, 2)),
            pltpu.SemaphoreType.DMA((2, nc, frames)),
            pltpu.SemaphoreType.DMA((2, 3, nc, frames)),
        ],
        compiler_params=pltpu.CompilerParams(
            collective_id=0, has_side_effects=True, vmem_limit_bytes=63 * 1024 * 1024
        ),
        cost_estimate=pl.CostEstimate(
            flops=4 * cells * depth * channels, bytes_accessed=4 * depth * channels, transcendentals=0
        ),
    )(
        inner(frames_in), inner(cache_first), gain_first[None], shift_first[None],
        kernel_first.reshape(depth, channels), bias_first[None],
        inner(cache_second), gain_second[None], shift_second[None],
        kernel_second.reshape(depth, channels), bias_second[None],
    )
    decoded, kept = pl.pallas_call(
        hand_over,
        out_shape=(
            jax.ShapeDtypeStruct(decoded.shape, BF16), jax.ShapeDtypeStruct(kept.shape, BF16),
        ),
        in_specs=[hbm, hbm],
        out_specs=(hbm, hbm),
        scratch_shapes=[
            pltpu.VMEM(decoded.shape, BF16), pltpu.VMEM(kept.shape, BF16),
            pltpu.SemaphoreType.DMA((frames + past,)), pltpu.SemaphoreType.DMA((frames + past,)),
        ],
        compiler_params=pltpu.CompilerParams(vmem_limit_bytes=63 * 1024 * 1024),
    )(decoded, kept)
    return jnp.transpose(decoded, (3, 0, 1, 2)), jnp.transpose(kept, (3, 0, 1, 2))


def solution(mesh):
    tile = P("chan", None, ("grp", "rows"), None)
    taps = P(None, None, None, "chan", None)
    return jax.shard_map(
        functools.partial(local, mesh.shape["rows"], mesh.shape["chan"]),
        mesh=mesh,
        in_specs=(
            tile, tile, P("chan"), P("chan"), taps, P("chan"),
            tile, P("chan"), P("chan"), taps, P("chan"),
        ),
        out_specs=(tile, tile),
        check_vma=False,
    )
```

```python
import functools

import jax
import jax.numpy as jnp
from jax import lax
from jax.experimental import pallas as pl
from jax.experimental.pallas import tpu as pltpu
from jax.sharding import PartitionSpec as P

GROUPS = 32
MESH = pl.DeviceIdType.MESH
F32 = jnp.float32
BF16 = jnp.bfloat16


def kernel(
    nr, nc, channels,
    x_hbm, c1_hbm, g1_hbm, s1_hbm, k1_hbm, b1_hbm, c2_hbm, g2_hbm, s2_hbm, k2_hbm, b2_hbm,
    out_hbm, next_hbm,
    xv, cv, vecs, kept, w, x9, halo, mom, part, snd, rcv,
    loc_sem, out_sem, mom_send, mom_recv, halo_send, halo_recv, rs_send, rs_recv,
):
    frames, band, width, ch = xv.shape
    past = cv.shape[1]
    taps = 9 * ch
    cells = frames * band * width
    fb = 2 if frames % 2 == 0 else 1
    r = lax.axis_index("rows")
    c = lax.axis_index("chan")
    half_line = nc // 2
    side = c // half_line
    inner = 1 - 2 * side
    place_in = c * (1 - side) + (nc - 1 - c) * side
    border = (place_in + 1) // half_line

    def chunk_at(d):
        return d * (1 - side) + (nc - 1 - d) * side


    loads = [
        pltpu.make_async_copy(src, dst, loc_sem.at[i])
        for i, (src, dst) in enumerate((
            (x_hbm, xv), (c1_hbm, cv.at[0]), (k1_hbm, w.at[0]),
            (c2_hbm, cv.at[1]), (k2_hbm, w.at[1]),
            (g1_hbm, vecs.at[0]), (s1_hbm, vecs.at[1]), (b1_hbm, vecs.at[2]),
            (g2_hbm, vecs.at[3]), (s2_hbm, vecs.at[4]), (b2_hbm, vecs.at[5]),
        ))
    ]
    barrier = pltpu.get_barrier_semaphore()
    for o in range(1, nr):
        pl.semaphore_signal(
            barrier, inc=1, device_id={"rows": lax.rem(r + o, nr)}, device_id_type=MESH
        )

    @pl.when(c > 0)
    def _():
        pl.semaphore_signal(barrier, inc=1, device_id={"chan": c - 1}, device_id_type=MESH)

    @pl.when(c < nc - 1)
    def _():
        pl.semaphore_signal(barrier, inc=1, device_id={"chan": c + 1}, device_id_type=MESH)

    @pl.when(border == 0)
    def _():
        pl.semaphore_signal(
            barrier, inc=1, device_id={"chan": chunk_at(half_line)}, device_id_type=MESH
        )

    for d in range(half_line + 1, nc):
        @pl.when(border == 1)
        def _():
            pl.semaphore_signal(
                barrier, inc=1, device_id={"chan": chunk_at(d)}, device_id_type=MESH
            )

    for i in (0, 1, 3, *range(5, len(loads))):
        loads[i].start()

    def moment_copy(conv, o):
        return pltpu.make_async_remote_copy(
            src_ref=mom.at[conv, 0], dst_ref=mom.at[conv, o],
            send_sem=mom_send.at[conv, o], recv_sem=mom_recv.at[conv, o],
            device_id={"rows": lax.rem(r + o, nr)}, device_id_type=MESH,
        )

    def halo_copy(src, conv, kind, side):
        row, step = (band - 1, 1) if side == 0 else (0, nr - 1)
        span = pl.ds(0, past) if kind == 0 else pl.ds(past, frames)
        return pltpu.make_async_remote_copy(
            src_ref=src.at[:, row], dst_ref=halo.at[conv, side, span],
            send_sem=halo_send.at[conv, kind, side], recv_sem=halo_recv.at[conv, kind, side],
            device_id={"rows": lax.rem(r + step, nr)}, device_id_type=MESH,
        )

    def sends_halo(side):
        return r < nr - 1 if side == 0 else r > 0

    def gets_halo(side):
        return r > 0 if side == 0 else r < nr - 1

    def halo_start(src, conv, kind):
        for side in range(2):
            @pl.when(sends_halo(side))
            def _():
                halo_copy(src, conv, kind, side).start()

    def halo_wait(src, conv, kind):
        for side in range(2):
            @pl.when(gets_halo(side))
            def _():
                halo_copy(src, conv, kind, side).wait_recv()

    def halo_drain(src, conv, kind):
        for side in range(2):
            @pl.when(sends_halo(side))
            def _():
                halo_copy(src, conv, kind, side).wait_send()

    def sums_of(v):
        v = v.astype(F32)
        return jnp.sum(v, axis=0, keepdims=True), jnp.sum(v * v, axis=0, keepdims=True)

    def set_moments(conv, sums):
        mom[conv, 0] = jnp.concatenate([*sums, jnp.zeros((6, ch), F32)], axis=0)

    def statistics(conv):
        total = mom[conv, 0]
        for o in range(1, nr):
            moment_copy(conv, o).wait_recv()
            total = total + mom[conv, o]
        per_group = channels // GROUPS
        i = lax.broadcasted_iota(jnp.int32, (ch, ch), 0) // per_group
        j = lax.broadcasted_iota(jnp.int32, (ch, ch), 1) // per_group
        same = jnp.where(i == j, 1.0, 0.0).astype(BF16)
        high = total.astype(BF16)
        rest = total - high.astype(F32)
        middle = rest.astype(BF16)
        low = (rest - middle.astype(F32)).astype(BF16)
        thirds = jnp.concatenate([t.astype(F32) for t in (high, middle, low)], axis=0)
        thirds = jnp.dot(thirds.astype(BF16), same, preferred_element_type=F32)
        total = (thirds[16:24] + thirds[8:16]) + thirds[0:8]
        total = total * (1.0 / (per_group * cells * nr))
        average = total[0:1]
        return average, lax.rsqrt(total[1:2] - average * average + 1e-06)

    def place(conv, j, p, v):
        s = lax.broadcasted_iota(jnp.int32, (width, ch), 0)
        low = jnp.where(s == 0, 0.0, pltpu.roll(v, 1, 0))
        high = jnp.where(s == width - 1, 0.0, pltpu.roll(v, width - 1, 0))
        for ds, t in enumerate((low, v, high)):
            t = t.astype(BF16)
            for dr in range(3):
                if 0 <= p - dr < band:
                    first = (dr * 3 + ds) * ch
                    x9[conv, j, p - dr, :, first : first + ch] = t

    def row_of(src, conv, j, f, p):
        if p == 0:
            return halo[conv, 0, j]
        if p == band + 1:
            return halo[conv, 1, j]
        return src[f, p - 1]

    def inside(p, v):
        if p == 0:
            return jnp.where(r > 0, v, jnp.zeros_like(v))
        if p == band + 1:
            return jnp.where(r < nr - 1, v, jnp.zeros_like(v))
        return v

    def place_past(conv, sides):
        def body(f, _):
            for p in sides:
                v = row_of(cv.at[conv], conv, f, f, p).astype(F32)
                place(conv, f, p, inside(p, v))
            return 0

        lax.fori_loop(0, past, body, 0)

    def place_current(src, conv, gain, shift, stats, sides, first, keep=False):
        average, inverse = stats
        slope = 0.5 * inverse * vecs[gain]
        level = 0.5 * vecs[shift] - average * slope

        def body(f, _):
            for p in sides:
                v = row_of(src, conv, f + past, f, p).astype(F32)
                u = v * slope + level
                v = (u + u * jnp.tanh(u)).astype(BF16)
                if keep:
                    @pl.when(f >= frames - past)
                    def _():
                        kept[f - (frames - past), p - 1] = v
                place(conv, f + past, p, inside(p, v.astype(F32)))
            return 0

        lax.fori_loop(first, first + fb, body, 0)

    own, edges = range(1, band + 1), (0, band + 1)
    gw = max(256, ch)
    ngroups = (nc * ch) // gw
    each = gw // ch
    mb = fb * band * width

    piece = band * width

    def multiply(conv, g, m):
        cols = pl.ds(pl.multiple_of(g * gw, gw), gw)
        lhs = jnp.concatenate(
            [x9[conv, pl.ds(m * fb + dt, fb)].reshape(mb, taps) for dt in range(3)], axis=1
        )
        acc = jnp.dot(lhs, w[conv, :, cols], preferred_element_type=F32)
        rows = pl.ds(pl.multiple_of(m * mb, mb), mb)
        for q in range(each):
            part[g * each + q, rows] = acc[:, q * ch : (q + 1) * ch]

    def rs_copy(conv, d, m, way, target):
        return pltpu.make_async_remote_copy(
            src_ref=snd.at[conv, d, m], dst_ref=rcv.at[conv, way, d, m],
            send_sem=rs_send.at[conv, d, m], recv_sem=rs_recv.at[conv, way, d, m],
            device_id={"chan": target}, device_id_type=MESH,
        )

    def sent_copy(conv, d, m, inward):
        if inward:
            target = border * d + (1 - border) * (c + inner)
            return rs_copy(conv, d, m, 2 * border, target)
        return rs_copy(conv, d, m, 1, c - inner)

    def rows_of(m):
        return pl.ds(pl.multiple_of(m * piece, piece), piece)

    def take(conv, d, m, way):
        rs_copy(conv, d, m, way, lax.rem(c + 1, nc)).wait_recv()
        part[d, rows_of(m)] = part[d, rows_of(m)] + rcv[conv, way, d, m].astype(F32)

    def emit(conv, spot, inward, start, count):
        d = chunk_at(spot)
        way, adds = (0, place_in > 0) if inward else (1, border == 0)

        def body(i, _):
            m = start + i

            @pl.when(adds)
            def _():
                take(conv, d, m, way)

            snd[conv, d, m] = part[d, rows_of(m)].astype(BF16)
            sent_copy(conv, d, m, inward).start()
            return 0

        lax.fori_loop(0, count, body, 0)

    def convolve(conv, bias, prepare, finish, meanwhile):
        start = (1 - side) * (ngroups // 2)
        half = ngroups // 2
        blocks = frames // fb

        def far_block(i, _):
            m = lax.rem(i, blocks)
            pl.when(i < blocks)(lambda: prepare(m))
            multiply(conv, lax.rem(start + i // blocks, ngroups), m)

            @pl.when((place_in == 0) & (i >= (half - 1) * blocks))
            def _():
                emit(conv, nc - 1, True, m * fb, fb)

            return 0

        def near_block(i, _):
            multiply(conv, lax.rem(start + half + i // blocks, ngroups), lax.rem(i, blocks))

            @pl.when((i == 0) & (place_in == 0))
            def _():
                for spot in range(nc - 2, half_line - 1, -1):
                    emit(conv, spot, True, 0, frames)

            @pl.when((i < blocks) & (place_in > 0))
            def _():
                emit(conv, nc - 1, True, i * fb, fb)

            return 0

        lax.fori_loop(0, half * blocks, far_block, 0)
        lax.fori_loop(0, (ngroups - half) * blocks, near_block, 0)

        for spot in range(half_line - 1):
            @pl.when(place_in > spot)
            def _():
                emit(conv, spot, False, 0, frames)

        for spot in range(nc - 2, 0, -1):
            @pl.when((place_in > 0) if spot >= half_line else (place_in < spot))
            def _():
                emit(conv, spot, True, 0, frames)

        meanwhile()

        def body(m, sums):
            for way, condition in ((1, border == 0), (0, place_in > 0)):
                @pl.when(condition)
                def _():
                    take(conv, c, m, way)

            take(conv, c, m, 2)
            v = (part[c, rows_of(m)] + vecs[bias]).astype(BF16)
            xv[m] = v.reshape(band, width, ch)
            finish(m)
            more = sums_of(v)
            return sums[0] + more[0], sums[1] + more[1]

        zero = jnp.zeros((1, ch), F32)
        return lax.fori_loop(0, frames, body, (zero, zero))

    def prepare(conv, gain, shift, stats, keep):
        def body(m):
            @pl.when(m > 0)
            def _():
                place_current(xv, conv, gain, shift, stats, own, m * fb, keep)

            place_current(xv, conv, gain, shift, stats, edges, m * fb)

        place_current(xv, conv, gain, shift, stats, own, 0, keep)
        halo_wait(xv, conv, 1)
        if conv == 0:
            halo_wait(cv.at[0], 0, 0)
            place_past(0, edges)
        return body

    def out_copy(f):
        return pltpu.make_async_copy(xv.at[f], out_hbm.at[f], out_sem.at[f])

    next_copy = pltpu.make_async_copy(kept, next_hbm, out_sem.at[frames])

    loads[0].wait()
    loads[2].start()
    set_moments(0, sums_of(xv[...].reshape(cells, ch)))
    pl.semaphore_wait(
        barrier,
        nr - 1 + jnp.where(c > 0, 1, 0) + jnp.where(c < nc - 1, 1, 0)
        + (1 - border) + border * (nc - half_line - 1),
    )
    for o in range(1, nr):
        moment_copy(0, o).start()
    halo_start(xv, 0, 1)
    loads[1].wait()
    halo_start(cv.at[0], 0, 0)
    place_past(0, own)
    for load in loads[5:]:
        load.wait()
    ready = prepare(0, 0, 1, statistics(0), False)
    loads[3].wait()
    halo_start(cv.at[1], 1, 0)
    loads[4].start()
    loads[2].wait()

    def early():
        halo_wait(cv.at[1], 1, 0)
        place_past(1, range(band + 2))
        halo_drain(xv, 0, 1)

    set_moments(1, convolve(0, 2, ready, lambda m: None, early))
    for o in range(1, nr):
        moment_copy(1, o).start()
    halo_start(xv, 1, 1)
    ready = prepare(1, 3, 4, statistics(1), True)
    loads[4].wait()

    def saved():
        next_copy.start()
        halo_drain(xv, 1, 1)

    convolve(1, 5, ready, lambda m: out_copy(m).start(), saved)
    for f in range(frames):
        out_copy(f).wait()
    next_copy.wait()

    halo_drain(cv.at[0], 0, 0)
    halo_drain(cv.at[1], 1, 0)
    for conv in range(2):
        for o in range(1, nr):
            moment_copy(conv, o).wait_send()
        for d in range(nc):
            @pl.when(c != d)
            def _():
                def body(m, _):
                    rs_copy(conv, d, m, 0, d).wait_send()
                    return 0

                lax.fori_loop(0, frames, body, 0)


def hand_over(a_hbm, b_hbm, c_hbm, d_hbm, a_held, b_held, in_sem, out_sem):
    copies = []
    for src, held, dst in ((a_hbm, a_held, c_hbm), (b_hbm, b_held, d_hbm)):
        for f in range(src.shape[0]):
            i = len(copies)
            copies.append((
                pltpu.make_async_copy(src.at[f], held.at[f], in_sem.at[i]),
                pltpu.make_async_copy(held.at[f], dst.at[f], out_sem.at[i]),
            ))
    for arrive, _ in copies:
        arrive.start()
    for arrive, leave in copies:
        arrive.wait()
        leave.start()
    for _, leave in copies:
        leave.wait()


def local(nr, nc, frames_in, cache_first, gain_first, shift_first, kernel_first, bias_first,
          cache_second, gain_second, shift_second, kernel_second, bias_second):
    def inner(a):
        return jnp.transpose(a, (1, 2, 3, 0))

    ch, frames, band, width = frames_in.shape
    past = cache_first.shape[1]
    channels = kernel_first.shape[4]
    depth = 27 * ch
    hbm = pl.BlockSpec(memory_space=pltpu.HBM)
    cells = frames * band * width
    decoded, kept = pl.pallas_call(
        functools.partial(kernel, nr, nc, channels),
        out_shape=(
            jax.ShapeDtypeStruct((frames, band, width, ch), BF16),
            jax.ShapeDtypeStruct((past, band, width, ch), BF16),
        ),
        in_specs=[hbm] * 11,
        out_specs=(hbm, hbm),
        scratch_shapes=[
            pltpu.VMEM((frames, band, width, ch), BF16),
            pltpu.VMEM((2, past, band, width, ch), BF16),
            pltpu.VMEM((6, 1, ch), F32),
            pltpu.VMEM((past, band, width, ch), BF16),
            pltpu.VMEM((2, depth, channels), BF16),
            pltpu.VMEM((2, past + frames, band, width, 9 * ch), BF16),
            pltpu.VMEM((2, 2, past + frames, width, ch), BF16),
            pltpu.VMEM((2, nr, 8, ch), F32),
            pltpu.VMEM((nc, cells, ch), F32),
            pltpu.VMEM((2, nc, frames, band * width, ch), BF16),
            pltpu.VMEM((2, 3, nc, frames, band * width, ch), BF16),
            pltpu.SemaphoreType.DMA((11,)),
            pltpu.SemaphoreType.DMA((frames + 1,)),
            pltpu.SemaphoreType.DMA((2, nr)),
            pltpu.SemaphoreType.DMA((2, nr)),
            pltpu.SemaphoreType.DMA((2, 2, 2)),
            pltpu.SemaphoreType.DMA((2, 2, 2)),
            pltpu.SemaphoreType.DMA((2, nc, frames)),
            pltpu.SemaphoreType.DMA((2, 3, nc, frames)),
        ],
        compiler_params=pltpu.CompilerParams(
            collective_id=0, has_side_effects=True, vmem_limit_bytes=63 * 1024 * 1024
        ),
        cost_estimate=pl.CostEstimate(
            flops=4 * cells * depth * channels, bytes_accessed=4 * depth * channels, transcendentals=0
        ),
    )(
        inner(frames_in), inner(cache_first), gain_first[None], shift_first[None],
        kernel_first.reshape(depth, channels), bias_first[None],
        inner(cache_second), gain_second[None], shift_second[None],
        kernel_second.reshape(depth, channels), bias_second[None],
    )
    decoded, kept = pl.pallas_call(
        hand_over,
        out_shape=(
            jax.ShapeDtypeStruct(decoded.shape, BF16), jax.ShapeDtypeStruct(kept.shape, BF16),
        ),
        in_specs=[hbm, hbm],
        out_specs=(hbm, hbm),
        scratch_shapes=[
            pltpu.VMEM(decoded.shape, BF16), pltpu.VMEM(kept.shape, BF16),
            pltpu.SemaphoreType.DMA((frames + past,)), pltpu.SemaphoreType.DMA((frames + past,)),
        ],
        compiler_params=pltpu.CompilerParams(vmem_limit_bytes=63 * 1024 * 1024),
    )(decoded, kept)
    return jnp.transpose(decoded, (3, 0, 1, 2)), jnp.transpose(kept, (3, 0, 1, 2))


def solution(mesh):
    tile = P("chan", None, ("grp", "rows"), None)
    taps = P(None, None, None, "chan", None)
    return jax.shard_map(
        functools.partial(local, mesh.shape["rows"], mesh.shape["chan"]),
        mesh=mesh,
        in_specs=(
            tile, tile, P("chan"), P("chan"), taps, P("chan"),
            tile, P("chan"), P("chan"), taps, P("chan"),
        ),
        out_specs=(tile, tile),
        check_vma=False,
    )
```

```python
import functools

import jax
import jax.numpy as jnp
from jax import lax
from jax.experimental import pallas as pl
from jax.experimental.pallas import tpu as pltpu
from jax.sharding import PartitionSpec as P

GROUPS = 32
MESH = pl.DeviceIdType.MESH
F32 = jnp.float32
BF16 = jnp.bfloat16


def kernel(
    nr, nc, channels,
    x_hbm, c1_hbm, g1_hbm, s1_hbm, k1_hbm, b1_hbm, c2_hbm, g2_hbm, s2_hbm, k2_hbm, b2_hbm,
    out_hbm, next_hbm,
    xv, cv, vecs, kept, w, x9, halo, mom, part, snd, rcv,
    loc_sem, out_sem, mom_send, mom_recv, halo_send, halo_recv, rs_send, rs_recv,
):
    frames, band, width, ch = xv.shape
    past = cv.shape[1]
    taps = 9 * ch
    cells = frames * band * width
    fb = 2 if frames % 2 == 0 else 1
    r = lax.axis_index("rows")
    c = lax.axis_index("chan")
    half_line = nc // 2
    side = c // half_line
    inner = 1 - 2 * side
    place_in = c * (1 - side) + (nc - 1 - c) * side
    border = (place_in + 1) // half_line

    def chunk_at(d):
        return d * (1 - side) + (nc - 1 - d) * side


    loads = [
        pltpu.make_async_copy(src, dst, loc_sem.at[i])
        for i, (src, dst) in enumerate((
            (x_hbm, xv), (c1_hbm, cv.at[0]), (k1_hbm, w.at[0]),
            (c2_hbm, cv.at[1]), (k2_hbm, w.at[1]),
            (g1_hbm, vecs.at[0]), (s1_hbm, vecs.at[1]), (b1_hbm, vecs.at[2]),
            (g2_hbm, vecs.at[3]), (s2_hbm, vecs.at[4]), (b2_hbm, vecs.at[5]),
        ))
    ]
    barrier = pltpu.get_barrier_semaphore()
    for o in range(1, nr):
        pl.semaphore_signal(
            barrier, inc=1, device_id={"rows": lax.rem(r + o, nr)}, device_id_type=MESH
        )

    @pl.when(c > 0)
    def _():
        pl.semaphore_signal(barrier, inc=1, device_id={"chan": c - 1}, device_id_type=MESH)

    @pl.when(c < nc - 1)
    def _():
        pl.semaphore_signal(barrier, inc=1, device_id={"chan": c + 1}, device_id_type=MESH)

    @pl.when(border == 0)
    def _():
        pl.semaphore_signal(
            barrier, inc=1, device_id={"chan": chunk_at(half_line)}, device_id_type=MESH
        )

    for d in range(half_line + 1, nc):
        @pl.when(border == 1)
        def _():
            pl.semaphore_signal(
                barrier, inc=1, device_id={"chan": chunk_at(d)}, device_id_type=MESH
            )

    for i in (0, 1, 3, *range(5, len(loads))):
        loads[i].start()

    def moment_copy(conv, o):
        return pltpu.make_async_remote_copy(
            src_ref=mom.at[conv, 0], dst_ref=mom.at[conv, o],
            send_sem=mom_send.at[conv, o], recv_sem=mom_recv.at[conv, o],
            device_id={"rows": lax.rem(r + o, nr)}, device_id_type=MESH,
        )

    def halo_copy(src, conv, kind, side):
        row, step = (band - 1, 1) if side == 0 else (0, nr - 1)
        span = pl.ds(0, past) if kind == 0 else pl.ds(past, frames)
        return pltpu.make_async_remote_copy(
            src_ref=src.at[:, row], dst_ref=halo.at[conv, side, span],
            send_sem=halo_send.at[conv, kind, side], recv_sem=halo_recv.at[conv, kind, side],
            device_id={"rows": lax.rem(r + step, nr)}, device_id_type=MESH,
        )

    def sends_halo(side):
        return r < nr - 1 if side == 0 else r > 0

    def gets_halo(side):
        return r > 0 if side == 0 else r < nr - 1

    def halo_start(src, conv, kind):
        for side in range(2):
            @pl.when(sends_halo(side))
            def _():
                halo_copy(src, conv, kind, side).start()

    def halo_wait(src, conv, kind):
        for side in range(2):
            @pl.when(gets_halo(side))
            def _():
                halo_copy(src, conv, kind, side).wait_recv()

    def halo_drain(src, conv, kind):
        for side in range(2):
            @pl.when(sends_halo(side))
            def _():
                halo_copy(src, conv, kind, side).wait_send()

    def sums_of(v):
        v = v.astype(F32)
        return jnp.sum(v, axis=0, keepdims=True), jnp.sum(v * v, axis=0, keepdims=True)

    def set_moments(conv, sums):
        mom[conv, 0] = jnp.concatenate([*sums, jnp.zeros((6, ch), F32)], axis=0)

    def statistics(conv):
        total = mom[conv, 0]
        for o in range(1, nr):
            moment_copy(conv, o).wait_recv()
            total = total + mom[conv, o]
        per_group = channels // GROUPS
        i = lax.broadcasted_iota(jnp.int32, (ch, ch), 0) // per_group
        j = lax.broadcasted_iota(jnp.int32, (ch, ch), 1) // per_group
        same = jnp.where(i == j, 1.0, 0.0).astype(BF16)
        high = total.astype(BF16)
        rest = total - high.astype(F32)
        middle = rest.astype(BF16)
        low = (rest - middle.astype(F32)).astype(BF16)
        thirds = jnp.concatenate([t.astype(F32) for t in (high, middle, low)], axis=0)
        thirds = jnp.dot(thirds.astype(BF16), same, preferred_element_type=F32)
        total = (thirds[16:24] + thirds[8:16]) + thirds[0:8]
        total = total * (1.0 / (per_group * cells * nr))
        average = total[0:1]
        return average, lax.rsqrt(total[1:2] - average * average + 1e-06)

    def place(conv, j, p, v):
        s = lax.broadcasted_iota(jnp.int32, (width, ch), 0)
        low = jnp.where(s == 0, 0.0, pltpu.roll(v, 1, 0))
        high = jnp.where(s == width - 1, 0.0, pltpu.roll(v, width - 1, 0))
        for ds, t in enumerate((low, v, high)):
            t = t.astype(BF16)
            for dr in range(3):
                if 0 <= p - dr < band:
                    first = (dr * 3 + ds) * ch
                    x9[conv, j, p - dr, :, first : first + ch] = t

    def row_of(src, conv, j, f, p):
        if p == 0:
            return halo[conv, 0, j]
        if p == band + 1:
            return halo[conv, 1, j]
        return src[f, p - 1]

    def inside(p, v):
        if p == 0:
            return jnp.where(r > 0, v, jnp.zeros_like(v))
        if p == band + 1:
            return jnp.where(r < nr - 1, v, jnp.zeros_like(v))
        return v

    def place_past(conv, sides):
        def body(f, _):
            for p in sides:
                v = row_of(cv.at[conv], conv, f, f, p).astype(F32)
                place(conv, f, p, inside(p, v))
            return 0

        lax.fori_loop(0, past, body, 0)

    def place_current(src, conv, gain, shift, stats, sides, first, keep=False):
        average, inverse = stats
        slope = 0.5 * inverse * vecs[gain]
        level = 0.5 * vecs[shift] - average * slope

        def body(f, _):
            for p in sides:
                v = row_of(src, conv, f + past, f, p).astype(F32)
                u = v * slope + level
                v = (u + u * jnp.tanh(u)).astype(BF16)
                if keep:
                    @pl.when(f >= frames - past)
                    def _():
                        kept[f - (frames - past), p - 1] = v
                place(conv, f + past, p, inside(p, v.astype(F32)))
            return 0

        lax.fori_loop(first, first + fb, body, 0)

    own, edges = range(1, band + 1), (0, band + 1)
    gw = max(256, ch)
    ngroups = (nc * ch) // gw
    each = gw // ch
    mb = fb * band * width

    piece = band * width

    def multiply(conv, g, m):
        cols = pl.ds(pl.multiple_of(g * gw, gw), gw)
        lhs = jnp.concatenate(
            [x9[conv, pl.ds(m * fb + dt, fb)].reshape(mb, taps) for dt in range(3)], axis=1
        )
        acc = jnp.dot(lhs, w[conv, :, cols], preferred_element_type=F32)
        rows = pl.ds(pl.multiple_of(m * mb, mb), mb)
        for q in range(each):
            part[g * each + q, rows] = acc[:, q * ch : (q + 1) * ch]

    def rs_copy(conv, d, m, way, target):
        return pltpu.make_async_remote_copy(
            src_ref=snd.at[conv, d, m], dst_ref=rcv.at[conv, way, d, m],
            send_sem=rs_send.at[conv, d, m], recv_sem=rs_recv.at[conv, way, d, m],
            device_id={"chan": target}, device_id_type=MESH,
        )

    def sent_copy(conv, d, m, inward):
        if inward:
            target = border * d + (1 - border) * (c + inner)
            return rs_copy(conv, d, m, 2 * border, target)
        return rs_copy(conv, d, m, 1, c - inner)

    def rows_of(m):
        return pl.ds(pl.multiple_of(m * piece, piece), piece)

    def take(conv, d, m, way):
        rs_copy(conv, d, m, way, lax.rem(c + 1, nc)).wait_recv()
        part[d, rows_of(m)] = part[d, rows_of(m)] + rcv[conv, way, d, m].astype(F32)

    def emit(conv, spot, inward, start, count):
        d = chunk_at(spot)
        way, adds = (0, place_in > 0) if inward else (1, border == 0)

        def body(i, _):
            m = start + i

            @pl.when(adds)
            def _():
                take(conv, d, m, way)

            snd[conv, d, m] = part[d, rows_of(m)].astype(BF16)
            sent_copy(conv, d, m, inward).start()
            return 0

        lax.fori_loop(0, count, body, 0)

    def convolve(conv, bias, prepare, finish, meanwhile):
        start = (1 - side) * (ngroups // 2)
        half = ngroups // 2
        blocks = frames // fb

        def far_block(i, _):
            m = lax.rem(i, blocks)
            pl.when(i < blocks)(lambda: prepare(m))
            multiply(conv, lax.rem(start + i // blocks, ngroups), m)

            @pl.when((place_in == 0) & (i >= (half - 1) * blocks))
            def _():
                emit(conv, nc - 1, True, m * fb, fb)

            return 0

        def near_block(i, _):
            multiply(conv, lax.rem(start + half + i // blocks, ngroups), lax.rem(i, blocks))

            @pl.when((i == 0) & (place_in == 0))
            def _():
                for spot in range(nc - 2, half_line - 1, -1):
                    emit(conv, spot, True, 0, frames)

            @pl.when((i < blocks) & (place_in > 0))
            def _():
                emit(conv, nc - 1, True, i * fb, fb)

            return 0

        lax.fori_loop(0, half * blocks, far_block, 0)
        lax.fori_loop(0, (ngroups - half) * blocks, near_block, 0)

        for spot in range(half_line - 1):
            @pl.when(place_in > spot)
            def _():
                emit(conv, spot, False, 0, frames)

        for spot in range(nc - 2, 0, -1):
            ready = (place_in > 0) if spot >= half_line else (place_in < spot)
            if conv == 0:
                ready = ready & (place_in > 0)

            @pl.when(ready)
            def _():
                emit(conv, spot, True, 0, frames)

        meanwhile()

        def body(m, sums):
            for way, condition in ((1, border == 0), (0, place_in > 0)):
                @pl.when(condition)
                def _():
                    take(conv, c, m, way)

            take(conv, c, m, 2)
            v = (part[c, rows_of(m)] + vecs[bias]).astype(BF16)
            xv[m] = v.reshape(band, width, ch)
            finish(m)
            more = sums_of(v)
            return sums[0] + more[0], sums[1] + more[1]

        zero = jnp.zeros((1, ch), F32)
        return lax.fori_loop(0, frames, body, (zero, zero))

    def prepare(conv, gain, shift, stats, keep):
        def body(m):
            @pl.when(m > 0)
            def _():
                place_current(xv, conv, gain, shift, stats, own, m * fb, keep)

            place_current(xv, conv, gain, shift, stats, edges, m * fb)

        place_current(xv, conv, gain, shift, stats, own, 0, keep)
        halo_wait(xv, conv, 1)
        if conv == 0:
            halo_wait(cv.at[0], 0, 0)
            place_past(0, edges)
        return body

    def out_copy(f):
        return pltpu.make_async_copy(xv.at[f], out_hbm.at[f], out_sem.at[f])

    next_copy = pltpu.make_async_copy(kept, next_hbm, out_sem.at[frames])

    loads[0].wait()
    loads[2].start()
    set_moments(0, sums_of(xv[...].reshape(cells, ch)))
    pl.semaphore_wait(
        barrier,
        nr - 1 + jnp.where(c > 0, 1, 0) + jnp.where(c < nc - 1, 1, 0)
        + (1 - border) + border * (nc - half_line - 1),
    )
    for o in range(1, nr):
        moment_copy(0, o).start()
    halo_start(xv, 0, 1)
    loads[1].wait()
    halo_start(cv.at[0], 0, 0)
    place_past(0, own)
    for load in loads[5:]:
        load.wait()
    ready = prepare(0, 0, 1, statistics(0), False)
    loads[3].wait()
    halo_start(cv.at[1], 1, 0)
    loads[4].start()
    loads[2].wait()

    def early():
        halo_wait(cv.at[1], 1, 0)
        place_past(1, range(band + 2))
        halo_drain(xv, 0, 1)

    set_moments(1, convolve(0, 2, ready, lambda m: None, early))
    for o in range(1, nr):
        moment_copy(1, o).start()
    halo_start(xv, 1, 1)

    @pl.when(place_in == 0)
    def _():
        for spot in range(half_line - 1, 0, -1):
            emit(0, spot, True, 0, frames)

    ready = prepare(1, 3, 4, statistics(1), True)
    loads[4].wait()

    def saved():
        next_copy.start()
        halo_drain(xv, 1, 1)

    convolve(1, 5, ready, lambda m: out_copy(m).start(), saved)
    for f in range(frames):
        out_copy(f).wait()
    next_copy.wait()

    halo_drain(cv.at[0], 0, 0)
    halo_drain(cv.at[1], 1, 0)
    for conv in range(2):
        for o in range(1, nr):
            moment_copy(conv, o).wait_send()
        for d in range(nc):
            @pl.when(c != d)
            def _():
                def body(m, _):
                    rs_copy(conv, d, m, 0, d).wait_send()
                    return 0

                lax.fori_loop(0, frames, body, 0)


def hand_over(a_hbm, b_hbm, c_hbm, d_hbm, a_held, b_held, in_sem, out_sem):
    copies = []
    for src, held, dst in ((a_hbm, a_held, c_hbm), (b_hbm, b_held, d_hbm)):
        for f in range(src.shape[0]):
            i = len(copies)
            copies.append((
                pltpu.make_async_copy(src.at[f], held.at[f], in_sem.at[i]),
                pltpu.make_async_copy(held.at[f], dst.at[f], out_sem.at[i]),
            ))
    for arrive, _ in copies:
        arrive.start()
    for arrive, leave in copies:
        arrive.wait()
        leave.start()
    for _, leave in copies:
        leave.wait()


def local(nr, nc, frames_in, cache_first, gain_first, shift_first, kernel_first, bias_first,
          cache_second, gain_second, shift_second, kernel_second, bias_second):
    def inner(a):
        return jnp.transpose(a, (1, 2, 3, 0))

    ch, frames, band, width = frames_in.shape
    past = cache_first.shape[1]
    channels = kernel_first.shape[4]
    depth = 27 * ch
    hbm = pl.BlockSpec(memory_space=pltpu.HBM)
    cells = frames * band * width
    decoded, kept = pl.pallas_call(
        functools.partial(kernel, nr, nc, channels),
        out_shape=(
            jax.ShapeDtypeStruct((frames, band, width, ch), BF16),
            jax.ShapeDtypeStruct((past, band, width, ch), BF16),
        ),
        in_specs=[hbm] * 11,
        out_specs=(hbm, hbm),
        scratch_shapes=[
            pltpu.VMEM((frames, band, width, ch), BF16),
            pltpu.VMEM((2, past, band, width, ch), BF16),
            pltpu.VMEM((6, 1, ch), F32),
            pltpu.VMEM((past, band, width, ch), BF16),
            pltpu.VMEM((2, depth, channels), BF16),
            pltpu.VMEM((2, past + frames, band, width, 9 * ch), BF16),
            pltpu.VMEM((2, 2, past + frames, width, ch), BF16),
            pltpu.VMEM((2, nr, 8, ch), F32),
            pltpu.VMEM((nc, cells, ch), F32),
            pltpu.VMEM((2, nc, frames, band * width, ch), BF16),
            pltpu.VMEM((2, 3, nc, frames, band * width, ch), BF16),
            pltpu.SemaphoreType.DMA((11,)),
            pltpu.SemaphoreType.DMA((frames + 1,)),
            pltpu.SemaphoreType.DMA((2, nr)),
            pltpu.SemaphoreType.DMA((2, nr)),
            pltpu.SemaphoreType.DMA((2, 2, 2)),
            pltpu.SemaphoreType.DMA((2, 2, 2)),
            pltpu.SemaphoreType.DMA((2, nc, frames)),
            pltpu.SemaphoreType.DMA((2, 3, nc, frames)),
        ],
        compiler_params=pltpu.CompilerParams(
            collective_id=0, has_side_effects=True, vmem_limit_bytes=63 * 1024 * 1024
        ),
        cost_estimate=pl.CostEstimate(
            flops=4 * cells * depth * channels, bytes_accessed=4 * depth * channels, transcendentals=0
        ),
    )(
        inner(frames_in), inner(cache_first), gain_first[None], shift_first[None],
        kernel_first.reshape(depth, channels), bias_first[None],
        inner(cache_second), gain_second[None], shift_second[None],
        kernel_second.reshape(depth, channels), bias_second[None],
    )
    decoded, kept = pl.pallas_call(
        hand_over,
        out_shape=(
            jax.ShapeDtypeStruct(decoded.shape, BF16), jax.ShapeDtypeStruct(kept.shape, BF16),
        ),
        in_specs=[hbm, hbm],
        out_specs=(hbm, hbm),
        scratch_shapes=[
            pltpu.VMEM(decoded.shape, BF16), pltpu.VMEM(kept.shape, BF16),
            pltpu.SemaphoreType.DMA((frames + past,)), pltpu.SemaphoreType.DMA((frames + past,)),
        ],
        compiler_params=pltpu.CompilerParams(vmem_limit_bytes=63 * 1024 * 1024),
    )(decoded, kept)
    return jnp.transpose(decoded, (3, 0, 1, 2)), jnp.transpose(kept, (3, 0, 1, 2))


def solution(mesh):
    tile = P("chan", None, ("grp", "rows"), None)
    taps = P(None, None, None, "chan", None)
    return jax.shard_map(
        functools.partial(local, mesh.shape["rows"], mesh.shape["chan"]),
        mesh=mesh,
        in_specs=(
            tile, tile, P("chan"), P("chan"), taps, P("chan"),
            tile, P("chan"), P("chan"), taps, P("chan"),
        ),
        out_specs=(tile, tile),
        check_vma=False,
    )
```
